32 devices in a mesh: tm: 16 (over z, y, core), space: 2 (over x).
Axes of the slice: x: 2, y: 2, z: 4, core: 2. Of those that a mesh axis runs over, the one named last changes fastest.
Arguments:
- model: float32 [16, 2048, 1024], P('tm', 'space'), may hold values from -6 to 6
- kernels: float32 [3, 600, 2048], P(None, None, ('space', 'tm')), may hold values from -0.078125 to 0.078125
Outputs:
- data: float32 [16, 600, 1024], P('tm', None, 'space')
The draws below stay inside these ranges and needn't reach their ends.
All inputs are finite; a program needn't handle non-finite values.
Results may differ from the reference program's by a relative error of at most 0.0003.
Values sent between devices are 32-bit elements; how exact they have to be, the bound alone decides.
No kernel may reach another device: no remote copies, remote signals or barrier semaphores. Data moves between devices by JAX's collectives and lax.ppermute only.
A program may use at most 64 MiB of HBM per device.

```python
import jax
import jax.numpy as jnp
from jax import lax

S = 600
COLS = 1024
LAGS = 3
TIMES = 16
P_SIZE = 2048


def raised(values, rng, source, target, parts, factor):
    owner, partner = [(jnp.arange(values.shape[position]) // (values.shape[position] // parts)).reshape([-1 if axis == position else 1 for axis in range(values.ndim)]) for position in (source, target)]
    chosen = jax.random.permutation(rng, parts)[partner]
    strong = (owner == chosen) | (owner == (partner + parts // 2) % parts)
    return jnp.where(strong, factor * values, values)


def block_levels(key, dims, split, smallest, top_value):
    level = 1.0
    for position, shards_of in split:
        steps = jax.random.uniform(jax.random.fold_in(jax.random.fold_in(key, 6), position), (shards_of,), jnp.float32, smallest / len(split), top_value / len(split))
        level = level * jnp.repeat(jnp.exp(steps), dims[position] // shards_of).reshape((-1,) + (1,) * (len(dims) - 1 - position))
    return level


def noise(rng, dims, deviation, limit, cuts=(), kind=jnp.bfloat16):
    drawn = jax.random.normal(rng, dims, jnp.float32) * deviation
    if len(cuts) > 0:
        drawn = block_levels(rng, dims, cuts, -0.22, 0.18) * drawn
    return jnp.clip(drawn, min=-limit, max=limit).astype(kind)


def noise_with(key, shape, deviation, most, pieces, heavy, kind=jnp.bfloat16):
    values = deviation * jax.random.normal(key, shape, jnp.float32)
    if pieces:
        values = values * block_levels(key, shape, pieces, -0.22, 0.18)
    return jnp.clip(raised(values, jax.random.fold_in(key, 3), *heavy), -most, most).astype(kind)


def setup_inputs(seed: int = 0) -> dict:
    arg_keys = jax.random.split(jax.random.key(seed), 3)
    model = noise_with(arg_keys[0], (TIMES, P_SIZE, COLS), 1.0, 6.0, ((0, 16), (1, 2)), (1, 2, 2, 2.0), jnp.float32)
    kernels = noise(arg_keys[1], (LAGS, S, P_SIZE), (LAGS * P_SIZE) ** -0.5, 0.078125, ((2, 32),), jnp.float32)
    return {"model": model, "kernels": kernels}


def reference(model, kernels):
    def one_time(time_index):
        summed = jnp.zeros((S, COLS), jnp.float32)
        for lag_index in range(LAGS):
            source_time = jnp.maximum(time_index - lag_index, 0).astype(jnp.int32)
            model_block = lax.dynamic_index_in_dim(model, source_time, 0, keepdims=False)
            lag_term = jnp.dot(kernels[lag_index], model_block, precision=lax.Precision.HIGHEST, preferred_element_type=jnp.float32)
            summed = summed + jnp.where(time_index >= lag_index, lag_term, jnp.zeros_like(lag_term))
        return summed
    return lax.map(one_time, jnp.arange(TIMES, dtype=jnp.int32))
```

```python
import functools

import jax
import jax.numpy as jnp
from jax import lax
from jax.experimental import pallas as pl
from jax.experimental.pallas import tpu as pltpu
from jax.sharding import Mesh, PartitionSpec as P

F32, BF16 = jnp.float32, jnp.bfloat16
VMEM_LIMIT = 48 * 2**20


def split(values):
    high = values.astype(BF16)
    return high, (values - high.astype(F32)).astype(BF16)


def spread_kernel(half, core_ref, kt_ref, keep_ref, send_ref, scratch):
    core = core_ref[0]
    lags, _, sensors = kt_ref.shape
    for lag in range(lags):
        scratch[...] = kt_ref[lag].T
        low, high = scratch[:half, :], scratch[sensors - half :, :]
        keep_ref[lag] = jnp.where(core == 0, low, high)
        send_ref[lag] = jnp.where(core == 0, high, low)


def halves_kernel(core_ref, own_ref, other_ref, high_ref, low_ref):
    core = core_ref[0]
    high_ref[core], low_ref[core] = split(own_ref[...])
    high_ref[1 - core], low_ref[1 - core] = split(other_ref[...])


def product(kh, kl, mh, ml):
    dot = functools.partial(jnp.dot, preferred_element_type=F32)
    return dot(kh, mh) + (dot(kh, ml) + dot(kl, mh))


def fill(k_ref, kh, kl):
    chips, _, width = k_ref.shape
    for chip in range(chips):
        columns = slice(chip * width, (chip + 1) * width)
        kh[:, columns], kl[:, columns] = split(k_ref[chip])


def one_kernel(info, k_ref, mh, ml, keep_ref, send_ref, kh, kl):
    part = pl.program_id(0)

    @pl.when(part == 0)
    def _():
        fill(k_ref, kh, kl)

    total = product(kh[...], kl[...], mh[0], ml[0])

    @pl.when(part == 0)
    def _():
        keep_ref[...] = total

    @pl.when(part > 0)
    def _():
        send_ref[0] = total


def two_kernel(info, k1_ref, k2_ref, m1h, m1l, m0h, m0l, keep_ref, send_ref, k1h, k1l, k2h, k2l):
    part = pl.program_id(0)

    @pl.when(part == 0)
    def _():
        fill(k1_ref, k1h, k1l)
        fill(k2_ref, k2h, k2l)

    total = product(k1h[...], k1l[...], m1h[0], m1l[0]) + product(k2h[...], k2l[...], m0h[0], m0l[0])

    @pl.when(part == 0)
    def _():
        keep_ref[...] = total

    @pl.when(part > 0)
    def _():
        send_ref[0] = total


def own_kernel(info, k0_ref, k1_ref, mth, mtl, m0h, m0l, keep_ref, send_ref, chip_ref, cross_ref, k0h, k0l, k1h, k1l):
    turn, part = pl.program_id(0), pl.program_id(1)

    @pl.when((turn == 0) & (part == 0))
    def _():
        fill(k0_ref, k0h, k0l)
        fill(k1_ref, k1h, k1l)

    slot = lax.rem(info[0] + turn, 2)

    def store(total):
        @pl.when((turn == 0) & (part == 0))
        def _():
            keep_ref[...] = total

        @pl.when((turn == 0) & (part > 0))
        def _():
            send_ref[0] = total

        @pl.when((turn == 1) & (part == 0))
        def _():
            chip_ref[...] = total

        @pl.when((turn == 1) & (part > 0))
        def _():
            cross_ref[0] = total

    @pl.when(slot == 0)
    def _():
        store(product(k0h[...], k0l[...], mth[0], mtl[0]))

    @pl.when(slot == 1)
    def _():
        store(product(k0h[...], k0l[...], mth[0], mtl[0]) + product(k1h[...], k1l[...], m0h[0], m0l[0]))


def finish_kernel(core_ref, a1, a2, a3, b1, b2, b3, out_ref):
    core = core_ref[0]
    sensors, half = out_ref.shape[0], a1.shape[0]
    own = a1[...] + a2[...] + a3[...]
    other = b1[...] + b2[...] + b3[...]
    out_ref[:half, :] = jnp.where(core == 0, own, other)
    out_ref[half:, :] = jnp.where(core == 0, other, own)[2 * half - sensors :, :]


def on_device(model, kernels, chips, spaces):
    core, place = lax.axis_index("core"), lax.axis_index("space")
    core_info = jnp.reshape(core, (1,)).astype(jnp.int32)
    info = jnp.stack([core, place]).astype(jnp.int32)
    own_model = model[0]
    depth, columns = own_model.shape
    lags, sensors, width = kernels.shape
    half = -(-sensors // 16) * 8
    block = columns // spaces
    params = pltpu.CompilerParams(vmem_limit_bytes=VMEM_LIMIT)
    smem = pl.BlockSpec(memory_space=pltpu.SMEM)
    vmem = pl.BlockSpec(memory_space=pltpu.VMEM)

    def swap(values):
        return lax.ppermute(values, "core", [(0, 1), (1, 0)])

    def onward(values):
        return lax.ppermute(values, "chip", [(i, i + 1) for i in range(chips - 1)])

    keep, send = pl.pallas_call(
        functools.partial(spread_kernel, half),
        out_shape=[jax.ShapeDtypeStruct((lags, half, width), F32)] * 2,
        in_specs=[smem, vmem],
        out_specs=[vmem, vmem],
        scratch_shapes=[pltpu.VMEM((sensors, width), F32)],
        compiler_params=params,
        name="spread",
    )(core_info, jnp.swapaxes(kernels, 1, 2))
    received = swap(send)
    first, second = jnp.where(core == 0, keep, received), jnp.where(core == 0, received, keep)
    chip_columns = jnp.concatenate([first, second], axis=2)
    k2, k1, k0 = [lax.all_gather(chip_columns[lag], "chip") for lag in (2, 1, 0)]

    rows = 256
    high, low = pl.pallas_call(
        halves_kernel,
        grid=(depth // rows,),
        out_shape=[jax.ShapeDtypeStruct((2, depth, columns), BF16)] * 2,
        in_specs=[smem] + [pl.BlockSpec((rows, columns), lambda i: (i, 0))] * 2,
        out_specs=[pl.BlockSpec((2, rows, columns), lambda i: (0, i, 0))] * 2,
        compiler_params=params,
        name="halves",
    )(core_info, own_model, swap(own_model))

    gathered = (chips, half, 2 * width)
    k_scratch = [pltpu.VMEM((half, depth), BF16)] * 2
    block_shape = jax.ShapeDtypeStruct((half, block), F32)
    sent_shape = jax.ShapeDtypeStruct((spaces - 1, half, block), F32)

    def m_spec(slot):
        return pl.BlockSpec((1, depth, block), lambda d, info: (slot, 0, lax.rem(info[1] + d, spaces)))

    def k_spec():
        return pl.BlockSpec(gathered, lambda *_: (0, 0, 0))

    out_specs = [
        pl.BlockSpec((half, block), lambda d, info: (0, 0)),
        pl.BlockSpec((1, half, block), lambda d, info: (jnp.maximum(d - 1, 0), 0, 0)),
    ]

    def flops(terms):
        return pl.CostEstimate(
            flops=terms * 6 * half * depth * columns, bytes_accessed=terms * 4 * depth * columns, transcendentals=0
        )

    o1_keep, o1_send = pl.pallas_call(
        one_kernel,
        grid_spec=pltpu.PrefetchScalarGridSpec(
            num_scalar_prefetch=1,
            grid=(spaces,),
            in_specs=[k_spec(), m_spec(1), m_spec(1)],
            out_specs=out_specs,
            scratch_shapes=k_scratch,
        ),
        out_shape=[block_shape, sent_shape],
        compiler_params=params,
        cost_estimate=flops(1),
        name="second_next",
    )(info, k2, high, low)
    o0_keep, o0_send = pl.pallas_call(
        two_kernel,
        grid_spec=pltpu.PrefetchScalarGridSpec(
            num_scalar_prefetch=1,
            grid=(spaces,),
            in_specs=[k_spec(), k_spec(), m_spec(1), m_spec(1), m_spec(0), m_spec(0)],
            out_specs=out_specs,
            scratch_shapes=k_scratch * 2,
        ),
        out_shape=[block_shape, sent_shape],
        compiler_params=params,
        cost_estimate=flops(2),
        name="first_next",
    )(info, k1, k2, high, low, high, low)

    def own_m_spec():
        return pl.BlockSpec(
            (1, depth, block),
            lambda turn, d, info: (lax.rem(info[0] + turn, 2), 0, lax.rem(info[1] + d, spaces)),
        )

    def zero_m_spec():
        return pl.BlockSpec((1, depth, block), lambda turn, d, info: (0, 0, lax.rem(info[1] + d, spaces)))

    def sent_index(owner):
        def index(turn, d, info):
            at = jnp.maximum(d - 1, 0)
            if owner == 0:
                return jnp.where(turn == 0, at, spaces - 2), 0, 0
            return jnp.where(turn == 1, at, 0), 0, 0

        return index

    kept_index = lambda turn, d, info: (0, 0)
    d_keep, d_send, d_chip, d_cross = pl.pallas_call(
        own_kernel,
        grid_spec=pltpu.PrefetchScalarGridSpec(
            num_scalar_prefetch=1,
            grid=(2, spaces),
            in_specs=[k_spec(), k_spec(), own_m_spec(), own_m_spec(), zero_m_spec(), zero_m_spec()],
            out_specs=[
                pl.BlockSpec((half, block), kept_index),
                pl.BlockSpec((1, half, block), sent_index(0)),
                pl.BlockSpec((half, block), kept_index),
                pl.BlockSpec((1, half, block), sent_index(1)),
            ],
            scratch_shapes=k_scratch * 2,
        ),
        out_shape=[block_shape, sent_shape, block_shape, sent_shape],
        compiler_params=params,
        cost_estimate=flops(3),
        name="own_times",
    )(info, k0, k1, high, low, high, low)

    def over_space(sent):
        parts = [
            lax.ppermute(sent[d - 1], "space", [(i, (i + d) % spaces) for i in range(spaces)])
            for d in range(1, spaces)
        ]
        return functools.reduce(jnp.add, parts)

    def over_space_and_core(sent):
        parts = [
            lax.ppermute(
                sent[d - 1],
                ("core", "space"),
                [(c * spaces + i, (1 - c) * spaces + (i + d) % spaces) for c in range(2) for i in range(spaces)],
            )
            for d in range(1, spaces)
        ]
        return functools.reduce(jnp.add, parts)

    next1 = onward(o1_keep + over_space(o1_send))
    next0 = onward(o0_keep + over_space(o0_send))
    next_own = jnp.where(core == 0, next0, next1)
    next_other = swap(jnp.where(core == 0, next1, next0))
    result = pl.pallas_call(
        finish_kernel,
        out_shape=jax.ShapeDtypeStruct((sensors, block), F32),
        in_specs=[smem] + [vmem] * 6,
        out_specs=vmem,
        compiler_params=params,
        name="finish",
    )(core_info, d_keep, next_own, over_space(d_send), swap(d_chip), next_other, over_space_and_core(d_cross))
    return result[None]


def solution(mesh):
    times, spaces = mesh.shape["tm"], mesh.shape["space"]
    chips = times // 2
    chip_mesh = Mesh(mesh.devices.reshape(chips, 2, spaces), ("chip", "core", "space"))
    return jax.shard_map(
        functools.partial(on_device, chips=chips, spaces=spaces),
        mesh=chip_mesh,
        in_specs=(P(("chip", "core"), "space", None), P(None, None, ("space", "chip", "core"))),
        out_specs=P(("chip", "core"), None, "space"),
        check_vma=False,
    )
```

```python
import functools

import jax
import jax.numpy as jnp
from jax import lax
from jax.experimental import pallas as pl
from jax.experimental.pallas import tpu as pltpu
from jax.sharding import Mesh, PartitionSpec as P

F32, BF16 = jnp.float32, jnp.bfloat16
VMEM_LIMIT = 28 * 2**20
SMEM_SPEC = pl.BlockSpec(memory_space=pltpu.SMEM)
VMEM_SPEC = pl.BlockSpec(memory_space=pltpu.VMEM)


def after(values, *others):
    return lax.optimization_barrier((values, *others))[0]


def split(values):
    high = values.astype(BF16)
    return high, (values - high.astype(F32)).astype(BF16)


def call(kernel, name, shapes, operands, flops=0):
    return pl.pallas_call(
        kernel,
        out_shape=shapes,
        in_specs=[SMEM_SPEC] + [VMEM_SPEC] * (len(operands) - 1),
        out_specs=[VMEM_SPEC] * len(shapes),
        compiler_params=pltpu.CompilerParams(vmem_limit_bytes=VMEM_LIMIT),
        cost_estimate=pl.CostEstimate(flops=flops, bytes_accessed=2**20, transcendentals=0),
        name=name,
    )(*operands)


def spread_kernel(info, own_ref, other_ref, *lag_refs):
    first = info[0] == 0
    half = lag_refs[0].shape[0]
    sensors = own_ref.shape[2]
    for lag, out_ref in enumerate(lag_refs):
        own, other = own_ref[lag], other_ref[lag]
        both = jnp.concatenate([jnp.where(first, own, other), jnp.where(first, other, own)], axis=0).T
        out_ref[...] = jnp.where(first, both[:half], both[sensors - half :])


def halves_kernel(info, own_ref, other_ref, high_ref, low_ref):
    core, place = info[0], info[1]
    spaces, block = high_ref.shape[1], high_ref.shape[3]
    for turn in range(spaces):
        columns = pl.ds(pl.multiple_of(lax.rem(place + turn, spaces) * block, block), block)
        high_ref[core, turn], low_ref[core, turn] = split(own_ref[:, columns])
        high_ref[1 - core, turn], low_ref[1 - core, turn] = split(other_ref[:, columns])


def chip_at(at, line, row, lines, rows):
    row_off, line_off = at // lines, at % lines
    return lax.rem(line - line_off + lines, lines) * rows + lax.rem(row + row_off, rows)


def fill(blocks, pair_ref):
    half, width = blocks[0].shape
    for at, block in enumerate(blocks):
        columns = slice(at * width, (at + 1) * width)
        pair_ref[:half, columns], pair_ref[half:, columns] = split(block[...])


def times(pair_ref, high_ref, low_ref, slot, turn, put):
    half = pair_ref.shape[0] // 2
    width = high_ref.shape[3]
    step = width if width % 256 else 256
    for start in range(0, width, step):
        columns = slice(start, start + step)
        both = jnp.dot(pair_ref[...], high_ref[slot, turn, :, columns], preferred_element_type=F32)
        low = jnp.dot(pair_ref[:half], low_ref[slot, turn, :, columns], preferred_element_type=F32)
        put(columns, both[:half] + (both[half:] + low))


def lead_two_kernel(info, high, low, *refs):
    blocks, (pair, send) = refs[:-2], refs[-2:]
    fill(blocks, pair)
    for turn in range(1, high.shape[1]):

        def put(columns, total):
            send[turn - 1, :, columns] = total

        times(pair, high, low, 1, turn, put)


def rest_kernel(info, high, low, pair, *refs):
    (*added, keep, other) = refs

    def put_keep(columns, total):
        keep[:, columns] = total + added[0][0, :, columns] if added else total

    times(pair, high, low, 1, 0, put_keep)
    for turn in range(high.shape[1]):

        def put(columns, total):
            other[turn, :, columns] = total

        times(pair, high, low, 0, turn, put)


def lead_one_kernel(info, high, low, added, *refs):
    blocks, (pair, send) = refs[:-2], refs[-2:]
    fill(blocks, pair)
    for turn in range(1, high.shape[1]):

        def put(columns, total):
            send[turn - 1, :, columns] = total + added[turn, :, columns]

        times(pair, high, low, 1, turn, put)


def both_times(info, high, low, pair, added, turn, own_put, other_put):
    first = info[0] == 0
    early = {}

    def put_early(columns, total):
        early[columns.start] = total

    def put_late(columns, total):
        late = total + added[turn, :, columns]
        own_put(columns, jnp.where(first, early[columns.start], late))
        other_put(columns, jnp.where(first, late, early[columns.start]))

    times(pair, high, low, 0, turn, put_early)
    times(pair, high, low, 1, turn, put_late)


def lead_zero_kernel(info, high, low, added, *refs):
    blocks, (pair, send, cross) = refs[:-3], refs[-3:]
    fill(blocks, pair)
    for turn in range(1, high.shape[1]):

        def own_put(columns, total):
            send[turn - 1, :, columns] = total

        def other_put(columns, total):
            cross[turn - 1, :, columns] = total

        both_times(info, high, low, pair, added, turn, own_put, other_put)


def last_kernel(info, high, low, pair, added, keep, chip):
    def own_put(columns, total):
        keep[:, columns] = total

    def other_put(columns, total):
        chip[:, columns] = total

    both_times(info, high, low, pair, added, 0, own_put, other_put)


def finish_kernel(info, a1, a2, a3, b1, b2, b3, out_ref):
    first = info[0] == 0
    sensors, half = out_ref.shape[0], a1.shape[0]
    own = a1[...] + a2[...] + a3[...]
    other = b1[...] + b2[...] + b3[...]
    out_ref[:half, :] = jnp.where(first, own, other)
    out_ref[half:, :] = jnp.where(first, other, own)[2 * half - sensors :, :]


def on_device(model, kernels, lines, rows, spaces):
    core = lax.axis_index("core")
    info = jnp.stack([core, lax.axis_index("space"), lax.axis_index("line"), lax.axis_index("row")]).astype(jnp.int32)
    own_model = model[0]
    depth, columns = own_model.shape
    lags, sensors, width = kernels.shape
    half = -(-sensors // 32) * 16
    block = columns // spaces

    def swap(values):
        return lax.ppermute(values, "core", [(0, 1), (1, 0)])

    def onward(values):
        return lax.ppermute(values, ("line", "row"), [(i, i + 1) for i in range(lines * rows - 1)])

    def over_space(sent):
        return [
            lax.ppermute(sent[d - 1], "space", [(i, (i + d) % spaces) for i in range(spaces)])
            for d in range(1, spaces)
        ]

    def over_space_and_core(sent):
        return [
            lax.ppermute(
                sent[d - 1],
                ("core", "space"),
                [(c * spaces + i, (1 - c) * spaces + (i + d) % spaces) for c in range(2) for i in range(spaces)],
            )
            for d in range(1, spaces)
        ]

    def total(parts):
        return functools.reduce(jnp.add, parts)

    kernels_t = jnp.swapaxes(kernels, 1, 2)
    other_t = swap(kernels_t)
    lag_blocks = call(
        spread_kernel, "spread", [jax.ShapeDtypeStruct((half, 2 * width), F32)] * lags, [info, kernels_t, other_t]
    )

    def arrived(at, info):
        return chip_at(at, info[2], info[3], lines, rows), 0

    high, low = pl.pallas_call(
        halves_kernel,
        grid_spec=pltpu.PrefetchScalarGridSpec(
            num_scalar_prefetch=1,
            grid=(lines * rows,),
            in_specs=[pl.BlockSpec((2 * width, columns), arrived)] * 2,
            out_specs=[pl.BlockSpec((2, spaces, 2 * width, block), lambda at, info: (0, 0, at, 0))] * 2,
        ),
        out_shape=[jax.ShapeDtypeStruct((2, spaces, depth, block), BF16)] * 2,
        compiler_params=pltpu.CompilerParams(vmem_limit_bytes=VMEM_LIMIT),
        name="halves",
    )(info, own_model, swap(after(own_model, other_t)))

    shifts = sorted(range(1, lines), key=lambda s: (min(s, lines - s), s))
    line_moves, row_moves = [], []

    def queued(moves, values, axis, route):
        if len(moves) >= 2:
            values = after(values, moves[-2])
        moved = lax.ppermute(values, axis, route)
        moves.append(moved)
        return moved

    gathered = {}
    for lag in (2, 1, 0):
        here = {0: lag_blocks[lag]}
        there = {}
        for shift in [0] + shifts:
            if shift:
                route = [(i, (i + shift) % lines) for i in range(lines)]
                here[shift] = queued(line_moves, lag_blocks[lag], "line", route)
            for off in range(1, rows):
                there[off, shift] = queued(
                    row_moves, here[shift], "row", [(i, (i - off) % rows) for i in range(rows)]
                )
        gathered[lag] = [here[s] for s in range(lines)] + [there[o, s] for o in range(1, rows) for s in range(lines)]

    pair = jax.ShapeDtypeStruct((2 * half, depth), BF16)
    one = jax.ShapeDtypeStruct((half, block), F32)
    sent = jax.ShapeDtypeStruct((spaces - 1, half, block), F32)
    whole = jax.ShapeDtypeStruct((spaces, half, block), F32)
    flops = 6 * half * depth * block

    pair2, send1 = call(lead_two_kernel, "lead2", [pair, sent], [info, high, low, *gathered[2]], flops)
    from1 = over_space(send1)
    keep1, early2 = call(rest_kernel, "rest2", [one, whole], [info, high, low, pair2], 3 * flops)

    pair1, send0 = call(lead_one_kernel, "lead1", [pair, sent], [info, high, low, early2, *gathered[1]], flops)
    from0 = over_space(send0)
    keep0, early1 = call(rest_kernel, "rest1", [one, whole], [info, high, low, pair1, early2], 3 * flops)

    pair0, d_send, d_cross = call(
        lead_zero_kernel, "lead0", [pair, sent, sent], [info, high, low, early1, *gathered[0]], 2 * flops
    )
    d_from, d_from_cross = over_space(d_send), over_space_and_core(d_cross)
    d_keep, d_chip = call(last_kernel, "last", [one, one], [info, high, low, pair0, early1], 2 * flops)

    next1 = onward(after(total([keep1, *from1]), row_moves[-1]))
    next0 = onward(after(total([keep0, *from0]), row_moves[-1]))
    next_own = jnp.where(core == 0, next0, next1)
    next_other = swap(jnp.where(core == 0, next1, next0))
    (result,) = call(
        finish_kernel,
        "finish",
        [jax.ShapeDtypeStruct((sensors, block), F32)],
        [info, d_keep, next_own, total(d_from), swap(d_chip), next_other, total(d_from_cross)],
    )
    return result[None]


def solution(mesh):
    chips, spaces = mesh.shape["tm"] // 2, mesh.shape["space"]
    rows = 1 if chips % 2 else 2
    lines = chips // rows
    grid = Mesh(mesh.devices.reshape(lines, rows, 2, spaces), ("line", "row", "core", "space"))
    return jax.shard_map(
        functools.partial(on_device, lines=lines, rows=rows, spaces=spaces),
        mesh=grid,
        in_specs=(P(("line", "row", "core"), "space", None), P(None, None, ("space", "line", "row", "core"))),
        out_specs=P(("line", "row", "core"), None, "space"),
        check_vma=False,
    )
```

```python
import functools

import jax
import jax.numpy as jnp
from jax import lax
from jax.experimental import pallas as pl
from jax.experimental.pallas import tpu as pltpu
from jax.sharding import Mesh, PartitionSpec as P

F32, BF16 = jnp.float32, jnp.bfloat16
VMEM_LIMIT = 28 * 2**20
SMEM_SPEC = pl.BlockSpec(memory_space=pltpu.SMEM)
VMEM_SPEC = pl.BlockSpec(memory_space=pltpu.VMEM)


def split(values):
    high = values.astype(BF16)
    return high, (values - high.astype(F32)).astype(BF16)


def call(kernel, name, shapes, operands, waits=(), flops=0, size=2**20, aliases=None):
    def body(*refs):
        kernel(*refs[: len(operands)], *refs[len(operands) + len(waits) :])

    return pl.pallas_call(
        body,
        out_shape=shapes,
        in_specs=[SMEM_SPEC] + [VMEM_SPEC] * (len(operands) - 1) + [pl.BlockSpec(memory_space=pl.ANY)] * len(waits),
        out_specs=[VMEM_SPEC] * len(shapes),
        input_output_aliases=aliases or {},
        compiler_params=pltpu.CompilerParams(vmem_limit_bytes=VMEM_LIMIT),
        cost_estimate=pl.CostEstimate(flops=flops, bytes_accessed=size, transcendentals=0),
        name=name,
    )(*operands, *waits)


def spread_kernel(info, own_ref, other_ref, *lag_refs):
    first = info[0] == 0
    half = lag_refs[0].shape[0]
    sensors = own_ref.shape[2]
    for lag, out_ref in enumerate(lag_refs):
        own, other = own_ref[lag], other_ref[lag]
        both = jnp.concatenate([jnp.where(first, own, other), jnp.where(first, other, own)], axis=0).T
        out_ref[...] = jnp.where(first, both[:half], both[sensors - half :])


def halves(info, model_ref, high_ref, low_ref, slot, lines, rows):
    spaces, depth, block = high_ref.shape[1:]
    width = depth // (lines * rows)
    for at in range(lines * rows):
        source = pl.ds(pl.multiple_of(chip_at(at, info, lines, rows) * width, width), width)
        target = slice(at * width, (at + 1) * width)
        for turn in range(spaces):
            columns = pl.ds(pl.multiple_of(lax.rem(info[1] + turn, spaces) * block, block), block)
            high_ref[slot, turn, target], low_ref[slot, turn, target] = split(model_ref[source, columns])


def own_halves_kernel(lines, rows, info, model_ref, far_ref, next_ref, high_ref, low_ref, far_out, next_out):
    far_out[...] = far_ref[...]
    next_out[...] = next_ref[...]
    halves(info, model_ref, high_ref, low_ref, info[0], lines, rows)


def other_halves_kernel(lines, rows, info, model_ref, high_in, low_in, high_ref, low_ref):
    halves(info, model_ref, high_ref, low_ref, 1 - info[0], lines, rows)


def line_shifts(lines):
    return [0] + sorted(range(1, lines), key=lambda shift: (min(shift, lines - shift), shift))


def chip_at(at, info, lines, rows):
    row_off, shift = at // lines, line_shifts(lines)[at % lines]
    return lax.rem(info[2] - shift + lines, lines) * rows + lax.rem(info[3] + row_off, rows)


def fill(blocks, pair_ref):
    half, width = pair_ref.shape[0] // 2, blocks[0].shape[1]
    at = 0
    for block in blocks:
        for start in range(0, block.shape[0], half):
            columns = slice(at * width, (at + 1) * width)
            pair_ref[:half, columns], pair_ref[half:, columns] = split(block[start : start + half])
            at += 1


def join_kernel(info, *refs):
    (*parts, out_ref) = refs
    start = 0
    for part in parts:
        out_ref[start : start + part.shape[0]] = part[...]
        start += part.shape[0]


def times(pair_ref, high_ref, low_ref, slot, turn, put):
    half = pair_ref.shape[0] // 2
    width = high_ref.shape[3]
    step = width if width % 256 else 256
    for start in range(0, width, step):
        columns = slice(start, start + step)
        both = jnp.dot(pair_ref[...], high_ref[slot, turn, :, columns], preferred_element_type=F32)
        low = jnp.dot(pair_ref[:half], low_ref[slot, turn, :, columns], preferred_element_type=F32)
        put(columns, both[:half] + (both[half:] + low))


def lead_two_kernel(info, high, low, next_block, *refs):
    blocks, (pair, send, next_out) = refs[:-3], refs[-3:]
    next_out[...] = next_block[...]
    fill(blocks, pair)
    for turn in range(1, high.shape[1]):

        def put(columns, total):
            send[turn - 1, :, columns] = total

        times(pair, high, low, 1, turn, put)


def rest_two_kernel(info, high, low, pair, keep, other):
    def put_keep(columns, total):
        keep[:, columns] = total

    times(pair, high, low, 1, 0, put_keep)
    for turn in range(high.shape[1]):

        def put(columns, total):
            other[turn, :, columns] = total

        times(pair, high, low, 0, turn, put)


def rest_one_kernel(info, high, low, pair, added, keep1, far, *refs):
    (*from1, keep, other, total1, far_out) = refs
    far_out[...] = far[...]
    total1[...] = functools.reduce(jnp.add, [keep1[...]] + [part[...] for part in from1])

    def put_keep(columns, total):
        keep[:, columns] = total + added[0, :, columns]

    times(pair, high, low, 1, 0, put_keep)
    for turn in range(high.shape[1]):

        def put(columns, total):
            other[turn, :, columns] = total

        times(pair, high, low, 0, turn, put)


def lead_one_kernel(count, info, high, low, added, *refs):
    blocks, next_blocks, (pair, send, next_out) = refs[: -count - 3], refs[-count - 3 : -3], refs[-3:]
    join_kernel(info, *next_blocks, next_out)
    fill(blocks, pair)
    for turn in range(1, high.shape[1]):

        def put(columns, total):
            send[turn - 1, :, columns] = total + added[turn, :, columns]

        times(pair, high, low, 1, turn, put)


def both_times(info, high, low, pair, added, turn, own_put, other_put):
    first = info[0] == 0
    early = {}

    def put_early(columns, total):
        early[columns.start] = total

    def put_late(columns, total):
        late = total + added[turn, :, columns]
        own_put(columns, jnp.where(first, early[columns.start], late))
        other_put(columns, jnp.where(first, late, early[columns.start]))

    times(pair, high, low, 0, turn, put_early)
    times(pair, high, low, 1, turn, put_late)


def lead_zero_kernel(info, high, low, added, *refs):
    blocks, (pair, send, cross) = refs[:-3], refs[-3:]
    fill(blocks, pair)
    for turn in range(1, high.shape[1]):

        def own_put(columns, total):
            send[turn - 1, :, columns] = total

        def other_put(columns, total):
            cross[turn - 1, :, columns] = total

        both_times(info, high, low, pair, added, turn, own_put, other_put)


def last_kernel(info, high, low, pair, added, keep, chip):
    def own_put(columns, total):
        keep[:, columns] = total

    def other_put(columns, total):
        chip[:, columns] = total

    both_times(info, high, low, pair, added, 0, own_put, other_put)


def totals_kernel(info, total1, keep0, *refs):
    (*from0, own_ref, other_ref) = refs
    first = info[0] == 0
    total0 = functools.reduce(jnp.add, [keep0[...]] + [part[...] for part in from0])
    own_ref[...] = jnp.where(first, total0, total1[...])
    other_ref[...] = jnp.where(first, total1[...], total0)


def finish_kernel(spaces, info, d_keep, d_chip, onward, *refs):
    (*parts, out_ref) = refs
    first = info[0] == 0
    sensors, half = out_ref.shape[0], d_keep.shape[0]
    own = d_keep[...] + onward[:half]
    other = d_chip[...] + onward[half:]
    for straight, cross in zip(parts[: spaces - 1], parts[spaces - 1 :]):
        own = own + straight[...]
        other = other + cross[...]
    out_ref[:half, :] = jnp.where(first, own, other)
    out_ref[half:, :] = jnp.where(first, other, own)[2 * half - sensors :, :]


def on_device(model, kernels, lines, rows, spaces):
    core = lax.axis_index("core")
    info = jnp.stack([core, lax.axis_index("space"), lax.axis_index("line"), lax.axis_index("row")]).astype(jnp.int32)
    own_model = model[0]
    depth, columns = own_model.shape
    lags, sensors, width = kernels.shape
    half = -(-sensors // 32) * 16
    block = columns // spaces

    def swap(values):
        return lax.ppermute(values, "core", [(0, 1), (1, 0)])

    def onward(values):
        return lax.ppermute(values, ("line", "row"), [(i, i + 1) for i in range(lines * rows - 1)])

    def over_space(sent):
        return [
            lax.ppermute(sent[d - 1], "space", [(i, (i + d) % spaces) for i in range(spaces)])
            for d in range(1, spaces)
        ]

    def over_space_and_core(sent):
        return [
            lax.ppermute(
                sent[d - 1],
                ("core", "space"),
                [(c * spaces + i, (1 - c) * spaces + (i + d) % spaces) for c in range(2) for i in range(spaces)],
            )
            for d in range(1, spaces)
        ]

    kernels_t = jnp.swapaxes(kernels, 1, 2)
    other_t = swap(kernels_t)
    lag_blocks = call(
        spread_kernel, "spread", [jax.ShapeDtypeStruct((half, 2 * width), F32)] * lags, [info, kernels_t, other_t]
    )

    def shifted(own_block):
        return [own_block] + [
            lax.ppermute(own_block, "line", [(i, (i + shift) % lines) for i in range(lines)])
            for shift in line_shifts(lines)[1:]
        ]

    def handed(blocks):
        return [
            lax.ppermute(values, "row", [(i, (i - off) % rows) for i in range(rows)])
            for off in range(1, rows)
            for values in blocks
        ]

    def joined(blocks, waits):
        shape = jax.ShapeDtypeStruct((half * len(blocks), blocks[0].shape[1]), F32)
        return call(join_kernel, "join", [shape], [info, *blocks], waits=waits)[0]

    pair = jax.ShapeDtypeStruct((2 * half, depth), BF16)
    one = jax.ShapeDtypeStruct((half, block), F32)
    sent = jax.ShapeDtypeStruct((spaces - 1, half, block), F32)
    whole = jax.ShapeDtypeStruct((spaces, half, block), F32)
    flops = 6 * half * depth * block

    line2 = shifted(lag_blocks[2])

    models = [jax.ShapeDtypeStruct((2, spaces, depth, block), BF16)] * 2
    small = jax.ShapeDtypeStruct((half, 2 * width), F32)
    late = min(2, lines - 1)
    high, low, late_block, block1 = call(
        functools.partial(own_halves_kernel, lines, rows),
        "own_halves",
        models + [small] * 2,
        [info, own_model, line2[late], lag_blocks[1]],
        size=1,
    )
    high, low = call(
        functools.partial(other_halves_kernel, lines, rows),
        "other_halves",
        models,
        [info, swap(own_model), high, low],
        size=1,
        aliases={2: 0, 3: 1},
    )
    row2 = handed(line2[:late] + [late_block] + line2[late + 1 :])
    pair2, send1, block0 = call(
        lead_two_kernel,
        "lead2",
        [pair, sent, small],
        [info, high, low, lag_blocks[0], *line2, *row2],
        flops=flops,
    )
    from1 = over_space(send1)
    keep1, early2 = call(rest_two_kernel, "rest2", [one, whole], [info, high, low, pair2], flops=3 * flops)

    line1, line0 = shifted(block1), shifted(block0)
    row1 = handed([joined(line1[:-1] or line1, [send1])] + line1[1:][-1:])
    near = line0[:-1] or line0
    pair1, send0, near0 = call(
        functools.partial(lead_one_kernel, len(near)),
        "lead1",
        [pair, sent, jax.ShapeDtypeStruct((half * len(near), 2 * width), F32)],
        [info, high, low, early2, *line1, *row1, *near],
        waits=from1,
        flops=flops,
    )
    from0 = over_space(send0)
    keep0, early1, total1, far0 = call(
        rest_one_kernel,
        "rest1",
        [one, whole, one, small],
        [info, high, low, pair1, early2, keep1, line0[-1], *from1],
        flops=3 * flops,
    )

    row0 = handed([near0, far0] if lines > 1 else [near0])
    pair0, d_send, d_cross = call(
        lead_zero_kernel, "lead0", [pair, sent, sent], [info, high, low, early1, *line0, *row0], flops=2 * flops
    )
    d_from, d_from_cross = over_space(d_send), over_space_and_core(d_cross)
    next_same, next_cross = call(totals_kernel, "totals", [one, one], [info, total1, keep0, *from0], waits=row0[-1:])
    arrived = onward(joined([next_same, swap(next_cross)], [d_send]))
    d_keep, d_chip = call(last_kernel, "last", [one, one], [info, high, low, pair0, early1], flops=2 * flops)
    (result,) = call(
        functools.partial(finish_kernel, spaces),
        "finish",
        [jax.ShapeDtypeStruct((sensors, block), F32)],
        [info, d_keep, swap(d_chip), arrived, *d_from, *d_from_cross],
    )
    return result[None]


def solution(mesh):
    chips, spaces = mesh.shape["tm"] // 2, mesh.shape["space"]
    rows = 1 if chips % 2 else 2
    lines = chips // rows
    grid = Mesh(mesh.devices.reshape(lines, rows, 2, spaces), ("line", "row", "core", "space"))
    return jax.shard_map(
        functools.partial(on_device, lines=lines, rows=rows, spaces=spaces),
        mesh=grid,
        in_specs=(P(("line", "row", "core"), "space", None), P(None, None, ("space", "line", "row", "core"))),
        out_specs=P(("line", "row", "core"), None, "space"),
        check_vma=False,
    )
```

```python
import functools

import jax
import jax.numpy as jnp
from jax import lax
from jax.experimental import pallas as pl
from jax.experimental.pallas import tpu as pltpu
from jax.sharding import Mesh, PartitionSpec as P

F32, BF16 = jnp.float32, jnp.bfloat16
VMEM_LIMIT = 28 * 2**20
SMEM_SPEC = pl.BlockSpec(memory_space=pltpu.SMEM)
VMEM_SPEC = pl.BlockSpec(memory_space=pltpu.VMEM)


def split(values):
    high = values.astype(BF16)
    return high, (values - high.astype(F32)).astype(BF16)


def call(kernel, name, shapes, operands, waits=(), flops=0, size=2**20, aliases=None, outside=(), scratch=()):
    def body(*refs):
        kernel(*refs[: len(operands)], *refs[len(operands) + len(waits) :])

    anywhere = pl.BlockSpec(memory_space=pl.ANY)
    specs = [SMEM_SPEC] + [pl.BlockSpec(memory_space=pltpu.HBM) if at in outside else VMEM_SPEC for at in range(1, len(operands))]

    return pl.pallas_call(
        body,
        out_shape=shapes,
        in_specs=specs + [anywhere] * len(waits),
        out_specs=[VMEM_SPEC] * len(shapes),
        scratch_shapes=list(scratch),
        input_output_aliases=aliases or {},
        compiler_params=pltpu.CompilerParams(vmem_limit_bytes=VMEM_LIMIT),
        cost_estimate=pl.CostEstimate(flops=flops, bytes_accessed=size, transcendentals=0),
        name=name,
    )(*operands, *waits)


def stage_kernel(info, source_ref, out_ref, done):
    copy = pltpu.make_async_copy(source_ref, out_ref, done)
    copy.start()
    copy.wait()


def spread_kernel(info, own_ref, other_ref, model_ref, *refs):
    (*lag_refs, model_out, done) = refs
    copy = pltpu.make_async_copy(model_ref, model_out, done)
    copy.start()
    first = info[0] == 0
    half = lag_refs[0].shape[0]
    sensors = own_ref.shape[2]
    for lag, out_ref in enumerate(lag_refs):
        own, other = own_ref[lag], other_ref[lag]
        both = jnp.concatenate([jnp.where(first, own, other), jnp.where(first, other, own)], axis=0).T
        out_ref[...] = jnp.where(first, both[:half], both[sensors - half :])
    copy.wait()


def halves(info, model_ref, high_ref, low_ref, slot, lines, rows):
    spaces, depth, block = high_ref.shape[1:]
    width = depth // (lines * rows)
    for at in range(lines * rows):
        source = pl.ds(pl.multiple_of(chip_at(at, info, lines, rows) * width, width), width)
        target = slice(at * width, (at + 1) * width)
        for turn in range(spaces):
            columns = pl.ds(pl.multiple_of(lax.rem(info[1] + turn, spaces) * block, block), block)
            high_ref[slot, turn, target], low_ref[slot, turn, target] = split(model_ref[source, columns])


def own_halves_kernel(lines, rows, info, model_ref, far_ref, next_ref, high_ref, low_ref, far_out, next_out):
    far_out[...] = far_ref[...]
    next_out[...] = next_ref[...]
    halves(info, model_ref, high_ref, low_ref, info[0], lines, rows)


def other_halves_kernel(lines, rows, info, model_ref, high_in, low_in, high_ref, low_ref):
    halves(info, model_ref, high_ref, low_ref, 1 - info[0], lines, rows)


def near_first(lines):
    return [0] + sorted(range(1, lines), key=lambda shift: (min(shift, lines - shift), shift))


def far_first(lines):
    return [0] + near_first(lines)[:0:-1]


def chip_at(at, info, lines, rows):
    row_off, shift = at // lines, at % lines
    return lax.rem(info[2] - shift + lines, lines) * rows + lax.rem(info[3] + row_off, rows)


def fill(blocks, shifts, pair_ref):
    half, width = pair_ref.shape[0] // 2, blocks[0].shape[1]
    count = 0
    for block in blocks:
        for start in range(0, block.shape[0], half):
            at = count // len(shifts) * len(shifts) + shifts[count % len(shifts)]
            columns = slice(at * width, (at + 1) * width)
            pair_ref[:half, columns], pair_ref[half:, columns] = split(block[start : start + half])
            count += 1


def join_kernel(info, *refs):
    (*parts, out_ref) = refs
    start = 0
    for part in parts:
        out_ref[start : start + part.shape[0]] = part[...]
        start += part.shape[0]


def times(pair_ref, high_ref, low_ref, slot, turn, put):
    half = pair_ref.shape[0] // 2
    width = high_ref.shape[3]
    step = width if width % 256 else 256
    for start in range(0, width, step):
        columns = slice(start, start + step)
        both = jnp.dot(pair_ref[...], high_ref[slot, turn, :, columns], preferred_element_type=F32)
        low = jnp.dot(pair_ref[:half], low_ref[slot, turn, :, columns], preferred_element_type=F32)
        put(columns, both[:half] + (both[half:] + low))


def lead_two_kernel(shifts, info, high, low, next_block, *refs):
    blocks, (pair, send, next_out) = refs[:-3], refs[-3:]
    next_out[...] = next_block[...]
    fill(blocks, shifts, pair)
    for turn in range(1, high.shape[1]):

        def put(columns, total):
            send[turn - 1, :, columns] = total

        times(pair, high, low, 1, turn, put)


def rest_two_kernel(info, high, low, pair, keep, other):
    def put_keep(columns, total):
        keep[:, columns] = total

    times(pair, high, low, 1, 0, put_keep)
    for turn in range(high.shape[1]):

        def put(columns, total):
            other[turn, :, columns] = total

        times(pair, high, low, 0, turn, put)


def rest_one_kernel(info, high, low, pair, added, keep1, *refs):
    (*from1, keep, other, total1) = refs
    total1[...] = functools.reduce(jnp.add, [keep1[...]] + [part[...] for part in from1])

    def put_keep(columns, total):
        keep[:, columns] = total + added[0, :, columns]

    times(pair, high, low, 1, 0, put_keep)
    for turn in range(high.shape[1]):

        def put(columns, total):
            other[turn, :, columns] = total

        times(pair, high, low, 0, turn, put)


def lead_one_kernel(shifts, count, info, high, low, added, *refs):
    if count:
        (*refs, next_out) = refs
        join_kernel(info, *refs[-count - 2 : -2], next_out)
    blocks, (pair, send) = refs[: len(refs) - count - 2], refs[-2:]
    fill(blocks, shifts, pair)
    for turn in range(1, high.shape[1]):

        def put(columns, total):
            send[turn - 1, :, columns] = total + added[turn, :, columns]

        times(pair, high, low, 1, turn, put)


def both_times(info, high, low, pair, added, turn, own_put, other_put):
    first = info[0] == 0
    early = {}

    def put_early(columns, total):
        early[columns.start] = total

    def put_late(columns, total):
        late = total + added[turn, :, columns]
        own_put(columns, jnp.where(first, early[columns.start], late))
        other_put(columns, jnp.where(first, late, early[columns.start]))

    times(pair, high, low, 0, turn, put_early)
    times(pair, high, low, 1, turn, put_late)


def lead_zero_kernel(shifts, info, high, low, added, *refs):
    blocks, (pair, send, cross, chip) = refs[:-4], refs[-4:]
    fill(blocks, shifts, pair)
    for turn in range(1, high.shape[1]):

        def own_put(columns, total):
            send[turn - 1, :, columns] = total

        def other_put(columns, total):
            cross[turn - 1, :, columns] = total

        both_times(info, high, low, pair, added, turn, own_put, other_put)
    later = jnp.where(info[0] == 0, 1.0, 0.0)

    def put(columns, total):
        chip[:, columns] = total + later * added[0, :, columns]

    times(pair, high, low, 1 - info[0], 0, put)


def last_kernel(info, high, low, pair, added, keep):
    later = jnp.where(info[0] == 0, 0.0, 1.0)

    def put(columns, total):
        keep[:, columns] = total + later * added[0, :, columns]

    times(pair, high, low, info[0], 0, put)


def totals_kernel(info, total1, keep0, *refs):
    (*from0, own_ref, other_ref) = refs
    first = info[0] == 0
    total0 = functools.reduce(jnp.add, [keep0[...]] + [part[...] for part in from0])
    own_ref[...] = jnp.where(first, total0, total1[...])
    other_ref[...] = jnp.where(first, total1[...], total0)


def finish_kernel(spaces, info, d_keep, d_chip, next_own, next_other, *refs):
    (*parts, out_ref) = refs
    first = info[0] == 0
    sensors, half = out_ref.shape[0], d_keep.shape[0]
    own = d_keep[...] + next_own[...]
    other = d_chip[...] + next_other[...]
    for straight, cross in zip(parts[: spaces - 1], parts[spaces - 1 :]):
        own = own + straight[...]
        other = other + cross[...]
    out_ref[:half, :] = jnp.where(first, own, other)
    out_ref[half:, :] = jnp.where(first, other, own)[2 * half - sensors :, :]


def on_device(model, kernels, lines, rows, spaces):
    core = lax.axis_index("core")
    info = jnp.stack([core, lax.axis_index("space"), lax.axis_index("line"), lax.axis_index("row")]).astype(jnp.int32)
    own_model = model[0]
    depth, columns = own_model.shape
    lags, sensors, width = kernels.shape
    half = -(-sensors // 32) * 16
    block = columns // spaces

    def swap(values):
        return lax.ppermute(values, "core", [(0, 1), (1, 0)])

    def onward(values):
        return lax.ppermute(values, ("line", "row"), [(i, i + 1) for i in range(lines * rows - 1)])

    def over_space(sent):
        return [
            lax.ppermute(sent[d - 1], "space", [(i, (i + d) % spaces) for i in range(spaces)])
            for d in range(1, spaces)
        ]

    def over_space_and_core(sent):
        return [
            lax.ppermute(
                sent[d - 1],
                ("core", "space"),
                [(c * spaces + i, (1 - c) * spaces + (i + d) % spaces) for c in range(2) for i in range(spaces)],
            )
            for d in range(1, spaces)
        ]

    kernels_t = jnp.swapaxes(kernels, 1, 2)
    copied = pltpu.SemaphoreType.DMA
    (own_t,) = call(
        stage_kernel,
        "stage",
        [jax.ShapeDtypeStruct(kernels_t.shape, F32)],
        [info, kernels_t],
        outside=[1],
        scratch=[copied],
    )
    small = jax.ShapeDtypeStruct((half, 2 * width), F32)
    *lag_blocks, staged = call(
        spread_kernel,
        "spread",
        [small] * lags + [jax.ShapeDtypeStruct(own_model.shape, F32)],
        [info, own_t, swap(kernels_t), own_model],
        outside=[3],
        scratch=[copied],
    )

    def shifted(own_block, shifts):
        return [own_block] + [
            lax.ppermute(own_block, "line", [(i, (i + shift) % lines) for i in range(lines)]) for shift in shifts[1:]
        ]

    def handed(blocks):
        return [
            lax.ppermute(values, "row", [(i, (i - off) % rows) for i in range(rows)])
            for off in range(1, rows)
            for values in blocks
        ]

    def joined(blocks, waits):
        shape = jax.ShapeDtypeStruct((half * len(blocks), blocks[0].shape[1]), F32)
        return call(join_kernel, "join", [shape], [info, *blocks], waits=waits)[0]

    pair = jax.ShapeDtypeStruct((2 * half, depth), BF16)
    one = jax.ShapeDtypeStruct((half, block), F32)
    sent = jax.ShapeDtypeStruct((spaces - 1, half, block), F32)
    whole = jax.ShapeDtypeStruct((spaces, half, block), F32)
    flops = 6 * half * depth * block

    orders = near_first(lines), far_first(lines)
    line2 = shifted(lag_blocks[2], orders[0])

    models = [jax.ShapeDtypeStruct((2, spaces, depth, block), BF16)] * 2
    late = min(2, lines - 1)
    high, low, late_block, block1 = call(
        functools.partial(own_halves_kernel, lines, rows),
        "own_halves",
        models + [small] * 2,
        [info, staged, line2[late], lag_blocks[1]],
        size=1,
    )
    high, low = call(
        functools.partial(other_halves_kernel, lines, rows),
        "other_halves",
        models,
        [info, swap(staged), high, low],
        size=1,
        aliases={2: 0, 3: 1},
    )
    row2 = handed(line2[:late] + [late_block] + line2[late + 1 :])
    line1 = shifted(block1, orders[1])
    pair2, send1, block0 = call(
        functools.partial(lead_two_kernel, orders[0]),
        "lead2",
        [pair, sent, small],
        [info, high, low, lag_blocks[0], *line2, *row2],
        waits=line1[1:2],
        flops=flops,
    )
    from1 = over_space(send1)
    keep1, early2 = call(rest_two_kernel, "rest2", [one, whole], [info, high, low, pair2], flops=3 * flops)

    line0 = shifted(block0, orders[1])

    def parts(line):
        return [part for part in (line[:1], line[1:-1], line[1:][-1:]) if part]

    row1 = handed([part[0] if len(part) == 1 else joined(part, [send1]) for part in parts(line1)])
    between = line0[1:-1]
    pair1, send0, *near0 = call(
        functools.partial(lead_one_kernel, orders[1], len(between)),
        "lead1",
        [pair, sent] + [jax.ShapeDtypeStruct((half * len(between), 2 * width), F32)] * bool(between),
        [info, high, low, early2, *line1, *row1, *between],
        waits=from1,
        flops=flops,
    )
    from0 = over_space(send0)
    row0 = handed(line0[:1] + near0 + line0[1:][-1:])
    keep0, early1, total1 = call(
        rest_one_kernel,
        "rest1",
        [one, whole, one],
        [info, high, low, pair1, early2, keep1, *from1],
        waits=row0[:2],
        flops=3 * flops,
    )
    pair0, d_send, d_cross, d_chip = call(
        functools.partial(lead_zero_kernel, orders[1]),
        "lead0",
        [pair, sent, sent, one],
        [info, high, low, early1, *line0, *row0],
        flops=3 * flops,
    )
    d_from, d_from_cross = over_space(d_send), over_space_and_core(d_cross)
    next_same, next_cross = call(totals_kernel, "totals", [one, one], [info, total1, keep0, *from0], waits=row0[-1:])
    (d_keep,) = call(last_kernel, "last", [one], [info, high, low, pair0, early1], flops=flops)
    (result,) = call(
        functools.partial(finish_kernel, spaces),
        "finish",
        [jax.ShapeDtypeStruct((sensors, block), F32)],
        [info, d_keep, swap(d_chip), onward(next_same), onward(swap(next_cross)), *d_from, *d_from_cross],
    )
    return result[None]


def solution(mesh):
    chips, spaces = mesh.shape["tm"] // 2, mesh.shape["space"]
    rows = 1 if chips % 2 else 2
    lines = chips // rows
    grid = Mesh(mesh.devices.reshape(lines, rows, 2, spaces), ("line", "row", "core", "space"))
    return jax.shard_map(
        functools.partial(on_device, lines=lines, rows=rows, spaces=spaces),
        mesh=grid,
        in_specs=(P(("line", "row", "core"), "space", None), P(None, None, ("space", "line", "row", "core"))),
        out_specs=P(("line", "row", "core"), None, "space"),
        check_vma=False,
    )
```

```python
import functools

import jax
import jax.numpy as jnp
from jax import lax
from jax.experimental import pallas as pl
from jax.experimental.pallas import tpu as pltpu
from jax.sharding import Mesh, PartitionSpec as P

F32, BF16 = jnp.float32, jnp.bfloat16
VMEM_LIMIT = 28 * 2**20
SMEM_SPEC = pl.BlockSpec(memory_space=pltpu.SMEM)
VMEM_SPEC = pl.BlockSpec(memory_space=pltpu.VMEM)


def split(values):
    high = values.astype(BF16)
    return high, (values - high.astype(F32)).astype(BF16)


def call(kernel, name, shapes, operands, waits=(), flops=0, aliases=None):
    def body(*refs):
        kernel(*refs[: len(operands)], *refs[len(operands) + len(waits) :])

    return pl.pallas_call(
        body,
        out_shape=shapes,
        in_specs=[SMEM_SPEC] + [VMEM_SPEC] * (len(operands) - 1) + [pl.BlockSpec(memory_space=pl.ANY)] * len(waits),
        out_specs=[VMEM_SPEC] * len(shapes),
        input_output_aliases=aliases or {},
        compiler_params=pltpu.CompilerParams(vmem_limit_bytes=VMEM_LIMIT),
        cost_estimate=pl.CostEstimate(flops=flops, bytes_accessed=1, transcendentals=0),
        name=name,
    )(*operands, *waits)


def stage_kernel(info, source_ref, out_ref):
    out_ref[...] = source_ref[...]


def spread_kernel(info, own_ref, other_ref, *lag_refs):
    first = info[0] == 0
    half = lag_refs[0].shape[0]
    sensors = own_ref.shape[2]
    for lag, out_ref in enumerate(lag_refs):
        own, other = own_ref[lag], other_ref[lag]
        both = jnp.concatenate([jnp.where(first, own, other), jnp.where(first, other, own)], axis=0).T
        out_ref[...] = jnp.where(first, both[:half], both[sensors - half :])


def own_halves_kernel(lines, rows, info, model_ref, next_ref, high_ref, low_ref, next_out, *staged_refs):
    next_out[...] = next_ref[...]
    spaces, depth, block = high_ref.shape[1:]
    width = depth // (lines * rows)
    for turn, staged_ref in enumerate(staged_refs):
        columns = pl.ds(pl.multiple_of(lax.rem(info[1] + turn, spaces) * block, block), block)
        for at in range(lines * rows):
            source = pl.ds(pl.multiple_of(chip_at(at, info, lines, rows) * width, width), width)
            target = slice(at * width, (at + 1) * width)
            values = model_ref[source, columns]
            staged_ref[target, :] = values
            high_ref[info[0], turn, target], low_ref[info[0], turn, target] = split(values)


def other_halves_kernel(info, high_in, low_in, *refs):
    (*staged_refs, high_ref, low_ref) = refs
    for turn, staged_ref in enumerate(staged_refs):
        high_ref[1 - info[0], turn], low_ref[1 - info[0], turn] = split(staged_ref[...])


def near_first(lines):
    return [0] + sorted(range(1, lines), key=lambda shift: (min(shift, lines - shift), shift))


def chip_at(at, info, lines, rows):
    row_off, shift = at // lines, at % lines
    return lax.rem(info[2] - shift + lines, lines) * rows + lax.rem(info[3] + row_off, rows)


def fill(lines, blocks, pair_ref):
    half, width = pair_ref.shape[0] // 2, blocks[0].shape[1]
    count = 0
    for block in blocks:
        for start in range(0, block.shape[0], half):
            at = count // lines * lines + near_first(lines)[count % lines]
            columns = slice(at * width, (at + 1) * width)
            pair_ref[:half, columns], pair_ref[half:, columns] = split(block[start : start + half])
            count += 1


def join_kernel(info, *refs):
    (*parts, out_ref) = refs
    start = 0
    for part in parts:
        out_ref[start : start + part.shape[0]] = part[...]
        start += part.shape[0]


def times(pair_ref, high_ref, low_ref, slot, turn, put):
    half = pair_ref.shape[0] // 2
    width = high_ref.shape[3]
    step = width if width % 256 else 256
    for start in range(0, width, step):
        columns = slice(start, start + step)
        both = jnp.dot(pair_ref[...], high_ref[slot, turn, :, columns], preferred_element_type=F32)
        low = jnp.dot(pair_ref[:half], low_ref[slot, turn, :, columns], preferred_element_type=F32)
        put(columns, both[:half] + (both[half:] + low))


def lead_two_kernel(lines, count, info, high, low, next_block, *refs):
    (*refs, next_out) = refs
    next_out[...] = next_block[...]
    blocks, (pair, send) = lead(lines, count, refs)
    for turn in range(1, high.shape[1]):

        def put(columns, total):
            send[turn - 1, :, columns] = total

        times(pair, high, low, 1, turn, put)


def lead(lines, count, refs):
    if count:
        (*refs, next_out) = refs
    outputs = refs[-2:]
    blocks, between = refs[: len(refs) - count - 2], refs[len(refs) - count - 2 : -2]
    if count:
        join_kernel(None, *between, next_out)
    fill(lines, blocks, outputs[0])
    return blocks, outputs


def rest_two_kernel(info, high, low, pair, keep, other):
    def put_keep(columns, total):
        keep[:, columns] = total

    times(pair, high, low, 1, 0, put_keep)
    for turn in range(high.shape[1]):

        def put(columns, total):
            other[turn, :, columns] = total

        times(pair, high, low, 0, turn, put)


def rest_one_kernel(info, high, low, pair, added, keep1, *refs):
    (*from1, keep, other, total1) = refs
    total1[...] = functools.reduce(jnp.add, [keep1[...]] + [part[...] for part in from1])

    def put_keep(columns, total):
        keep[:, columns] = total + added[0, :, columns]

    times(pair, high, low, 1, 0, put_keep)
    for turn in range(high.shape[1]):

        def put(columns, total):
            other[turn, :, columns] = total

        times(pair, high, low, 0, turn, put)


def lead_one_kernel(lines, count, info, high, low, added, *refs):
    blocks, (pair, send) = lead(lines, count, refs)
    for turn in range(1, high.shape[1]):

        def put(columns, total):
            send[turn - 1, :, columns] = total + added[turn, :, columns]

        times(pair, high, low, 1, turn, put)


def both_times(info, high, low, pair, added, turn, own_put, other_put):
    first = info[0] == 0
    early = {}

    def put_early(columns, total):
        early[columns.start] = total

    def put_late(columns, total):
        late = total + added[turn, :, columns]
        own_put(columns, jnp.where(first, early[columns.start], late))
        other_put(columns, jnp.where(first, late, early[columns.start]))

    times(pair, high, low, 0, turn, put_early)
    times(pair, high, low, 1, turn, put_late)


def lead_zero_kernel(lines, info, high, low, added, *refs):
    blocks, (pair, send, cross, chip) = refs[:-4], refs[-4:]
    fill(lines, blocks, pair)
    for turn in range(1, high.shape[1]):

        def own_put(columns, total):
            send[turn - 1, :, columns] = total

        def other_put(columns, total):
            cross[turn - 1, :, columns] = total

        both_times(info, high, low, pair, added, turn, own_put, other_put)
    later = jnp.where(info[0] == 0, 1.0, 0.0)

    def put(columns, total):
        chip[:, columns] = total + later * added[0, :, columns]

    times(pair, high, low, 1 - info[0], 0, put)


def last_kernel(info, high, low, pair, added, keep):
    later = jnp.where(info[0] == 0, 0.0, 1.0)

    def put(columns, total):
        keep[:, columns] = total + later * added[0, :, columns]

    times(pair, high, low, info[0], 0, put)


def totals_kernel(info, total1, keep0, *refs):
    (*from0, own_ref, other_ref) = refs
    first = info[0] == 0
    total0 = functools.reduce(jnp.add, [keep0[...]] + [part[...] for part in from0])
    own_ref[...] = jnp.where(first, total0, total1[...])
    other_ref[...] = jnp.where(first, total1[...], total0)


def finish_kernel(spaces, info, d_keep, d_chip, next_own, next_other, *refs):
    (*parts, out_ref) = refs
    first = info[0] == 0
    sensors, half = out_ref.shape[0], d_keep.shape[0]
    own = d_keep[...] + next_own[...]
    other = d_chip[...] + next_other[...]
    for straight, cross in zip(parts[: spaces - 1], parts[spaces - 1 :]):
        own = own + straight[...]
        other = other + cross[...]
    out_ref[:half, :] = jnp.where(first, own, other)
    out_ref[half:, :] = jnp.where(first, other, own)[2 * half - sensors :, :]


def on_device(model, kernels, lines, rows, spaces):
    core = lax.axis_index("core")
    info = jnp.stack([core, lax.axis_index("space"), lax.axis_index("line"), lax.axis_index("row")]).astype(jnp.int32)
    own_model = model[0]
    depth, columns = own_model.shape
    lags, sensors, width = kernels.shape
    half = -(-sensors // 32) * 16
    block = columns // spaces

    def swap(values):
        return lax.ppermute(values, "core", [(0, 1), (1, 0)])

    def onward(values):
        return lax.ppermute(values, ("line", "row"), [(i, i + 1) for i in range(lines * rows - 1)])

    def over_space(sent):
        return [
            lax.ppermute(sent[d - 1], "space", [(i, (i + d) % spaces) for i in range(spaces)])
            for d in range(1, spaces)
        ]

    def over_space_and_core(sent):
        return [
            lax.ppermute(
                sent[d - 1],
                ("core", "space"),
                [(c * spaces + i, (1 - c) * spaces + (i + d) % spaces) for c in range(2) for i in range(spaces)],
            )
            for d in range(1, spaces)
        ]

    kernels_t = jnp.swapaxes(kernels, 1, 2)
    (own_t,) = call(stage_kernel, "stage", [jax.ShapeDtypeStruct(kernels_t.shape, F32)], [info, kernels_t])
    small = jax.ShapeDtypeStruct((half, 2 * width), F32)
    lag_blocks = call(spread_kernel, "spread", [small] * lags, [info, own_t, swap(kernels_t)])

    def shifted(own_block):
        moved = [
            lax.ppermute(own_block, "line", [(i, (i + shift) % lines) for i in range(lines)])
            for shift in near_first(lines)[1:]
        ]
        return [own_block], moved[:-1], moved[-1:]

    def handed(blocks):
        return [
            lax.ppermute(values, "row", [(i, (i - off) % rows) for i in range(rows)])
            for off in range(1, rows)
            for values in blocks
        ]

    between = max(lines - 2, 0)
    joint = [jax.ShapeDtypeStruct((half * between, 2 * width), F32)] * bool(between)

    pair = jax.ShapeDtypeStruct((2 * half, depth), BF16)
    one = jax.ShapeDtypeStruct((half, block), F32)
    sent = jax.ShapeDtypeStruct((spaces - 1, half, block), F32)
    whole = jax.ShapeDtypeStruct((spaces, half, block), F32)
    flops = 6 * half * depth * block

    own2, near2, far2 = shifted(lag_blocks[2])
    row2 = handed(own2)

    models = [jax.ShapeDtypeStruct((2, spaces, depth, block), BF16)] * 2
    high, low, block1, *staged = call(
        functools.partial(own_halves_kernel, lines, rows),
        "own_halves",
        models + [small] + [jax.ShapeDtypeStruct((depth, block), F32)] * spaces,
        [info, own_model, lag_blocks[1]],
        waits=row2 + near2,
    )
    joint2 = call(join_kernel, "join2", joint, [info, *near2]) if joint else []
    high, low = call(
        other_halves_kernel,
        "other_halves",
        models,
        [info, high, low] + [swap(part) for part in staged],
        aliases={1: 0, 2: 1},
    )

    def gathered(own, near, far, row_own, near_joint):
        return own + near + far, ordered(row_own, handed(near_joint), handed(far))

    def ordered(*groups):
        each = [len(group) // (rows - 1) if rows > 1 else 0 for group in groups]
        return [
            group[off * size + at] for off in range(rows - 1) for group, size in zip(groups, each) for at in range(size)
        ]

    line2, row2 = gathered(own2, near2, far2, row2, joint2)
    own1, near1, far1 = shifted(block1)
    row_own1 = handed(own1)
    pair2, send1, *joint1, block0 = call(
        functools.partial(lead_two_kernel, lines, between),
        "lead2",
        [pair, sent] + joint + [small],
        [info, high, low, lag_blocks[0], *line2, *row2, *near1],
        waits=row_own1,
        flops=flops,
    )
    from1 = over_space(send1)
    line1, row1 = gathered(own1, near1, far1, row_own1, joint1)
    keep1, early2 = call(
        rest_two_kernel, "rest2", [one, whole], [info, high, low, pair2], waits=row1[:2], flops=3 * flops
    )
    own0, near0, far0 = shifted(block0)
    row_own0 = handed(own0)
    pair1, send0, *joint0 = call(
        functools.partial(lead_one_kernel, lines, between),
        "lead1",
        [pair, sent] + joint,
        [info, high, low, early2, *line1, *row1, *near0],
        waits=from1 + row_own0,
        flops=flops,
    )
    from0 = over_space(send0)
    line0, row0 = gathered(own0, near0, far0, row_own0, joint0)
    keep0, early1, total1 = call(
        rest_one_kernel,
        "rest1",
        [one, whole, one],
        [info, high, low, pair1, early2, keep1, *from1],
        waits=row0[:2],
        flops=3 * flops,
    )
    pair0, d_send, d_cross, d_chip = call(
        functools.partial(lead_zero_kernel, lines),
        "lead0",
        [pair, sent, sent, one],
        [info, high, low, early1, *line0, *row0],
        flops=3 * flops,
    )
    d_from, d_from_cross = over_space(d_send), over_space_and_core(d_cross)
    next_same, next_cross = call(totals_kernel, "totals", [one, one], [info, total1, keep0, *from0], waits=row0[-1:])
    (d_keep,) = call(last_kernel, "last", [one], [info, high, low, pair0, early1], flops=flops)
    (result,) = call(
        functools.partial(finish_kernel, spaces),
        "finish",
        [jax.ShapeDtypeStruct((sensors, block), F32)],
        [info, d_keep, swap(d_chip), onward(next_same), onward(swap(next_cross)), *d_from, *d_from_cross],
    )
    return result[None]


def solution(mesh):
    chips, spaces = mesh.shape["tm"] // 2, mesh.shape["space"]
    rows = 1 if chips % 2 else 2
    lines = chips // rows
    grid = Mesh(mesh.devices.reshape(lines, rows, 2, spaces), ("line", "row", "core", "space"))
    return jax.shard_map(
        functools.partial(on_device, lines=lines, rows=rows, spaces=spaces),
        mesh=grid,
        in_specs=(P(("line", "row", "core"), "space", None), P(None, None, ("space", "line", "row", "core"))),
        out_specs=P(("line", "row", "core"), None, "space"),
        check_vma=False,
    )
```

```python
import functools

import jax
import jax.numpy as jnp
from jax import lax
from jax.experimental import pallas as pl
from jax.experimental.pallas import tpu as pltpu
from jax.sharding import Mesh, PartitionSpec as P

F32, BF16 = jnp.float32, jnp.bfloat16
VMEM_LIMIT = 28 * 2**20
SMEM_SPEC = pl.BlockSpec(memory_space=pltpu.SMEM)
VMEM_SPEC = pl.BlockSpec(memory_space=pltpu.VMEM)


def split(values):
    high = values.astype(BF16)
    return high, (values - high.astype(F32)).astype(BF16)


def call(kernel, name, shapes, operands, waits=(), flops=0, aliases=None):
    def body(*refs):
        kernel(*refs[: len(operands)], *refs[len(operands) + len(waits) :])

    return pl.pallas_call(
        body,
        out_shape=shapes,
        in_specs=[SMEM_SPEC] + [VMEM_SPEC] * (len(operands) - 1) + [pl.BlockSpec(memory_space=pl.ANY)] * len(waits),
        out_specs=[VMEM_SPEC] * len(shapes),
        input_output_aliases=aliases or {},
        compiler_params=pltpu.CompilerParams(vmem_limit_bytes=VMEM_LIMIT),
        cost_estimate=pl.CostEstimate(flops=flops, bytes_accessed=1, transcendentals=0),
        name=name,
    )(*operands, *waits)


def stage_kernel(info, source_ref, out_ref):
    out_ref[...] = source_ref[...]


def spread_kernel(info, own_ref, other_ref, *lag_refs):
    first = info[0] == 0
    half = lag_refs[0].shape[0]
    sensors = own_ref.shape[2]
    for lag, out_ref in enumerate(lag_refs):
        own, other = own_ref[lag], other_ref[lag]
        both = jnp.concatenate([jnp.where(first, own, other), jnp.where(first, other, own)], axis=0).T
        out_ref[...] = jnp.where(first, both[:half], both[sensors - half :])


def own_halves_kernel(lines, rows, info, model_ref, next_ref, high_ref, low_ref, next_out, *staged_refs):
    next_out[...] = next_ref[...]
    spaces, depth, block = high_ref.shape[1:]
    width = depth // (lines * rows)
    for turn, staged_ref in enumerate(staged_refs):
        columns = pl.ds(pl.multiple_of(lax.rem(info[1] + turn, spaces) * block, block), block)
        for at in range(lines * rows):
            source = pl.ds(pl.multiple_of(chip_at(at, info, lines, rows) * width, width), width)
            target = slice(at * width, (at + 1) * width)
            values = model_ref[source, columns]
            staged_ref[target, :] = values
            high_ref[info[0], turn, target], low_ref[info[0], turn, target] = split(values)


def other_halves_kernel(info, high_in, low_in, *refs):
    (*staged_refs, high_ref, low_ref) = refs
    for turn, staged_ref in enumerate(staged_refs):
        high_ref[1 - info[0], turn], low_ref[1 - info[0], turn] = split(staged_ref[...])


def near_first(lines):
    return [0] + sorted(range(1, lines), key=lambda shift: (min(shift, lines - shift), shift))


def chip_at(at, info, lines, rows):
    row_off, shift = at // lines, at % lines
    return lax.rem(info[2] - shift + lines, lines) * rows + lax.rem(info[3] + row_off, rows)


def fill(lines, blocks, pair_ref):
    half, width = pair_ref.shape[0] // 2, blocks[0].shape[1]
    count = 0
    for block in blocks:
        for start in range(0, block.shape[0], half):
            at = count // lines * lines + near_first(lines)[count % lines]
            columns = slice(at * width, (at + 1) * width)
            pair_ref[:half, columns], pair_ref[half:, columns] = split(block[start : start + half])
            count += 1


def join_kernel(info, *refs):
    (*parts, out_ref) = refs
    start = 0
    for part in parts:
        out_ref[start : start + part.shape[0]] = part[...]
        start += part.shape[0]


def times(pair_ref, high_ref, low_ref, slot, turn, put):
    half = pair_ref.shape[0] // 2
    width = high_ref.shape[3]
    step = width if width % 256 else 256
    for start in range(0, width, step):
        columns = slice(start, start + step)
        both = jnp.dot(pair_ref[...], high_ref[slot, turn, :, columns], preferred_element_type=F32)
        low = jnp.dot(pair_ref[:half], low_ref[slot, turn, :, columns], preferred_element_type=F32)
        put(columns, both[:half] + (both[half:] + low))


def lead_two_kernel(lines, count, info, high, low, next_block, *refs):
    (*refs, next_out) = refs
    next_out[...] = next_block[...]
    blocks, (pair, send) = lead(lines, count, refs)
    for turn in range(1, high.shape[1]):

        def put(columns, total):
            send[turn - 1, :, columns] = total

        times(pair, high, low, 1, turn, put)


def lead(lines, count, refs):
    if count:
        (*refs, next_out) = refs
    outputs = refs[-2:]
    blocks, between = refs[: len(refs) - count - 2], refs[len(refs) - count - 2 : -2]
    if count:
        join_kernel(None, *between, next_out)
    fill(lines, blocks, outputs[0])
    return blocks, outputs


def rest_two_kernel(info, high, low, pair, keep, other):
    def put_keep(columns, total):
        keep[:, columns] = total

    times(pair, high, low, 1, 0, put_keep)
    for turn in range(high.shape[1]):

        def put(columns, total):
            other[turn, :, columns] = total

        times(pair, high, low, 0, turn, put)


def rest_one_kernel(info, high, low, pair, added, keep1, *refs):
    (*from1, keep, other, total1) = refs
    total1[...] = functools.reduce(jnp.add, [keep1[...]] + [part[...] for part in from1])

    def put_keep(columns, total):
        keep[:, columns] = total + added[0, :, columns]

    times(pair, high, low, 1, 0, put_keep)
    for turn in range(high.shape[1]):

        def put(columns, total):
            other[turn, :, columns] = total

        times(pair, high, low, 0, turn, put)


def lead_one_kernel(lines, count, info, high, low, added, *refs):
    blocks, (pair, send) = lead(lines, count, refs)
    for turn in range(1, high.shape[1]):

        def put(columns, total):
            send[turn - 1, :, columns] = total + added[turn, :, columns]

        times(pair, high, low, 1, turn, put)


def both_times(info, high, low, pair, added, turn, own_put, other_put):
    first = info[0] == 0
    early = {}

    def put_early(columns, total):
        early[columns.start] = total

    def put_late(columns, total):
        late = total + added[turn, :, columns]
        own_put(columns, jnp.where(first, early[columns.start], late))
        other_put(columns, jnp.where(first, late, early[columns.start]))

    times(pair, high, low, 0, turn, put_early)
    times(pair, high, low, 1, turn, put_late)


def lead_zero_kernel(lines, info, high, low, added, *refs):
    blocks, (pair, send, cross, chip) = refs[:-4], refs[-4:]
    fill(lines, blocks, pair)
    for turn in range(1, high.shape[1]):

        def own_put(columns, total):
            send[turn - 1, :, columns] = total

        def other_put(columns, total):
            cross[turn - 1, :, columns] = total

        both_times(info, high, low, pair, added, turn, own_put, other_put)
    later = jnp.where(info[0] == 0, 1.0, 0.0)

    def put(columns, total):
        chip[:, columns] = total + later * added[0, :, columns]

    times(pair, high, low, 1 - info[0], 0, put)


def last_kernel(info, high, low, pair, added, keep):
    later = jnp.where(info[0] == 0, 0.0, 1.0)

    def put(columns, total):
        keep[:, columns] = total + later * added[0, :, columns]

    times(pair, high, low, info[0], 0, put)


def totals_kernel(info, total1, keep0, *refs):
    (*from0, own_ref, other_ref) = refs
    first = info[0] == 0
    total0 = functools.reduce(jnp.add, [keep0[...]] + [part[...] for part in from0])
    own_ref[...] = jnp.where(first, total0, total1[...])
    other_ref[...] = jnp.where(first, total1[...], total0)


def finish_kernel(spaces, info, d_keep, d_chip, next_own, next_other, *refs):
    (*parts, out_ref) = refs
    first = info[0] == 0
    sensors, half = out_ref.shape[0], d_keep.shape[0]
    own = d_keep[...] + next_own[...]
    other = d_chip[...] + next_other[...]
    for straight, cross in zip(parts[: spaces - 1], parts[spaces - 1 :]):
        own = own + straight[...]
        other = other + cross[...]
    out_ref[:half, :] = jnp.where(first, own, other)
    out_ref[half:, :] = jnp.where(first, other, own)[2 * half - sensors :, :]


def on_device(model, kernels, lines, rows, spaces):
    core = lax.axis_index("core")
    info = jnp.stack([core, lax.axis_index("space"), lax.axis_index("line"), lax.axis_index("row")]).astype(jnp.int32)
    own_model = model[0]
    depth, columns = own_model.shape
    lags, sensors, width = kernels.shape
    half = -(-sensors // 32) * 16
    block = columns // spaces

    def swap(values):
        return lax.ppermute(values, "core", [(0, 1), (1, 0)])

    def onward(values):
        return lax.ppermute(values, ("line", "row"), [(i, i + 1) for i in range(lines * rows - 1)])

    def onward_across(values):
        route = [(2 * i + core, 2 * i + 3 - core) for i in range(lines * rows - 1) for core in range(2)]
        return lax.ppermute(values, ("line", "row", "core"), route)

    def over_space(sent):
        return [
            lax.ppermute(sent[d - 1], "space", [(i, (i + d) % spaces) for i in range(spaces)])
            for d in range(1, spaces)
        ]

    def over_space_and_core(sent):
        return [
            lax.ppermute(
                sent[d - 1],
                ("core", "space"),
                [(c * spaces + i, (1 - c) * spaces + (i + d) % spaces) for c in range(2) for i in range(spaces)],
            )
            for d in range(1, spaces)
        ]

    kernels_t = jnp.swapaxes(kernels, 1, 2)
    (own_t,) = call(stage_kernel, "stage", [jax.ShapeDtypeStruct(kernels_t.shape, F32)], [info, kernels_t])
    small = jax.ShapeDtypeStruct((half, 2 * width), F32)
    lag_blocks = call(spread_kernel, "spread", [small] * lags, [info, own_t, swap(kernels_t)])

    def shifted(own_block):
        held = {0: own_block, lines: own_block}
        for shift in near_first(lines)[1:]:
            step = 1 if shift <= lines - shift else -1
            held[shift] = lax.ppermute(held[shift - step], "line", [(i, (i + step) % lines) for i in range(lines)])
        moved = [held[shift] for shift in near_first(lines)[1:]]
        return [own_block], moved[:-1], moved[-1:]

    def handed(blocks):
        return [
            lax.ppermute(values, "row", [(i, (i - off) % rows) for i in range(rows)])
            for off in range(1, rows)
            for values in blocks
        ]

    between = max(lines - 2, 0)
    joint = [jax.ShapeDtypeStruct((half * between, 2 * width), F32)] * bool(between)

    pair = jax.ShapeDtypeStruct((2 * half, depth), BF16)
    one = jax.ShapeDtypeStruct((half, block), F32)
    sent = jax.ShapeDtypeStruct((spaces - 1, half, block), F32)
    whole = jax.ShapeDtypeStruct((spaces, half, block), F32)
    flops = 6 * half * depth * block

    own2, near2, far2 = shifted(lag_blocks[2])
    row2 = handed(own2)

    models = [jax.ShapeDtypeStruct((2, spaces, depth, block), BF16)] * 2
    high, low, block1, *staged = call(
        functools.partial(own_halves_kernel, lines, rows),
        "own_halves",
        models + [small] + [jax.ShapeDtypeStruct((depth, block), F32)] * spaces,
        [info, own_model, lag_blocks[1]],
    )
    joint2 = call(join_kernel, "join2", joint, [info, *near2], waits=row2) if joint else []
    high, low = call(
        other_halves_kernel,
        "other_halves",
        models,
        [info, high, low] + [swap(part) for part in staged],
        aliases={1: 0, 2: 1},
    )

    def gathered(own, near, far, row_own, near_joint):
        return own + near + far, ordered(row_own, handed(near_joint), handed(far))

    def ordered(*groups):
        each = [len(group) // (rows - 1) if rows > 1 else 0 for group in groups]
        return [
            group[off * size + at] for off in range(rows - 1) for group, size in zip(groups, each) for at in range(size)
        ]

    line2, row2 = gathered(own2, near2, far2, row2, joint2)
    own1, near1, far1 = shifted(block1)
    row_own1 = handed(own1)
    pair2, send1, *joint1, block0 = call(
        functools.partial(lead_two_kernel, lines, between),
        "lead2",
        [pair, sent] + joint + [small],
        [info, high, low, lag_blocks[0], *line2, *row2, *near1],
        waits=row_own1,
        flops=flops,
    )
    from1 = over_space(send1)
    line1, row1 = gathered(own1, near1, far1, row_own1, joint1)
    keep1, early2 = call(
        rest_two_kernel, "rest2", [one, whole], [info, high, low, pair2], waits=row1[:2], flops=3 * flops
    )
    own0, near0, far0 = shifted(block0)
    row_own0 = handed(own0)
    pair1, send0, *joint0 = call(
        functools.partial(lead_one_kernel, lines, between),
        "lead1",
        [pair, sent] + joint,
        [info, high, low, early2, *line1, *row1, *near0],
        waits=from1 + row_own0,
        flops=flops,
    )
    from0 = over_space(send0)
    line0, row0 = gathered(own0, near0, far0, row_own0, joint0)
    keep0, early1, total1 = call(
        rest_one_kernel,
        "rest1",
        [one, whole, one],
        [info, high, low, pair1, early2, keep1, *from1],
        waits=row0[:2],
        flops=3 * flops,
    )
    pair0, d_send, d_cross, d_chip = call(
        functools.partial(lead_zero_kernel, lines),
        "lead0",
        [pair, sent, sent, one],
        [info, high, low, early1, *line0, *row0],
        flops=3 * flops,
    )
    d_from, d_from_cross = over_space(d_send), over_space_and_core(d_cross)
    next_same, next_cross = call(totals_kernel, "totals", [one, one], [info, total1, keep0, *from0], waits=row0[-1:])
    (d_keep,) = call(last_kernel, "last", [one], [info, high, low, pair0, early1], flops=flops)
    (result,) = call(
        functools.partial(finish_kernel, spaces),
        "finish",
        [jax.ShapeDtypeStruct((sensors, block), F32)],
        [info, d_keep, swap(d_chip), onward(next_same), onward_across(next_cross), *d_from, *d_from_cross],
    )
    return result[None]


def solution(mesh):
    chips, spaces = mesh.shape["tm"] // 2, mesh.shape["space"]
    rows = 1 if chips % 2 else 2
    lines = chips // rows
    grid = Mesh(mesh.devices.reshape(lines, rows, 2, spaces), ("line", "row", "core", "space"))
    return jax.shard_map(
        functools.partial(on_device, lines=lines, rows=rows, spaces=spaces),
        mesh=grid,
        in_specs=(P(("line", "row", "core"), "space", None), P(None, None, ("space", "line", "row", "core"))),
        out_specs=P(("line", "row", "core"), None, "space"),
        check_vma=False,
    )
```

```python
import functools

import jax
import jax.numpy as jnp
from jax import lax
from jax.experimental import pallas as pl
from jax.experimental.pallas import tpu as pltpu
from jax.sharding import Mesh, PartitionSpec as P

F32, BF16 = jnp.float32, jnp.bfloat16
VMEM_LIMIT = 28 * 2**20
SMEM_SPEC = pl.BlockSpec(memory_space=pltpu.SMEM)
VMEM_SPEC = pl.BlockSpec(memory_space=pltpu.VMEM)


def split(values):
    high = values.astype(BF16)
    return high, (values - high.astype(F32)).astype(BF16)


def call(kernel, name, shapes, operands, waits=(), flops=0, aliases=None):
    def body(*refs):
        kernel(*refs[: len(operands)], *refs[len(operands) + len(waits) :])

    return pl.pallas_call(
        body,
        out_shape=shapes,
        in_specs=[SMEM_SPEC] + [VMEM_SPEC] * (len(operands) - 1) + [pl.BlockSpec(memory_space=pl.ANY)] * len(waits),
        out_specs=[VMEM_SPEC] * len(shapes),
        input_output_aliases=aliases or {},
        compiler_params=pltpu.CompilerParams(vmem_limit_bytes=VMEM_LIMIT),
        cost_estimate=pl.CostEstimate(flops=flops, bytes_accessed=1, transcendentals=0),
        name=name,
    )(*operands, *waits)


def stage_kernel(info, source_ref, out_ref):
    out_ref[...] = source_ref[...]


def spread_kernel(info, own_ref, other_ref, *lag_refs):
    first = info[0] == 0
    half = lag_refs[0].shape[0]
    sensors = own_ref.shape[2]
    for lag, out_ref in enumerate(lag_refs):
        own, other = own_ref[lag], other_ref[lag]
        both = jnp.concatenate([jnp.where(first, own, other), jnp.where(first, other, own)], axis=0).T
        out_ref[...] = jnp.where(first, both[:half], both[sensors - half :])


def own_halves_kernel(lines, rows, info, model_ref, next_ref, high_ref, low_ref, next_out, *staged_refs):
    next_out[...] = next_ref[...]
    spaces, depth, block = high_ref.shape[1:]
    width = depth // (lines * rows)
    for turn, staged_ref in enumerate(staged_refs):
        columns = pl.ds(pl.multiple_of(lax.rem(info[1] + turn, spaces) * block, block), block)
        for at in range(lines * rows):
            source = pl.ds(pl.multiple_of(chip_at(at, info, lines, rows) * width, width), width)
            target = slice(at * width, (at + 1) * width)
            values = model_ref[source, columns]
            staged_ref[target, :] = values
            high_ref[info[0], turn, target], low_ref[info[0], turn, target] = split(values)


def other_halves_kernel(info, high_in, low_in, *refs):
    (*staged_refs, high_ref, low_ref) = refs
    for turn, staged_ref in enumerate(staged_refs):
        high_ref[1 - info[0], turn], low_ref[1 - info[0], turn] = split(staged_ref[...])


def near_first(lines):
    return [0] + sorted(range(1, lines), key=lambda shift: (min(shift, lines - shift), shift))


def chip_at(at, info, lines, rows):
    row_off, shift = at // lines, at % lines
    return lax.rem(info[2] - shift + lines, lines) * rows + lax.rem(info[3] + row_off, rows)


def fill(lines, blocks, pair_ref):
    half, width = pair_ref.shape[0] // 2, blocks[0].shape[1]
    count = 0
    for block in blocks:
        for start in range(0, block.shape[0], half):
            at = count // lines * lines + near_first(lines)[count % lines]
            columns = slice(at * width, (at + 1) * width)
            pair_ref[:half, columns], pair_ref[half:, columns] = split(block[start : start + half])
            count += 1


def join_kernel(info, *refs):
    (*parts, out_ref) = refs
    start = 0
    for part in parts:
        out_ref[start : start + part.shape[0]] = part[...]
        start += part.shape[0]


def times(pair_ref, high_ref, low_ref, slot, turn, put):
    half = pair_ref.shape[0] // 2
    width = high_ref.shape[3]
    step = width if width % 256 else 256
    for start in range(0, width, step):
        columns = slice(start, start + step)
        both = jnp.dot(pair_ref[...], high_ref[slot, turn, :, columns], preferred_element_type=F32)
        low = jnp.dot(pair_ref[:half], low_ref[slot, turn, :, columns], preferred_element_type=F32)
        put(columns, both[:half] + (both[half:] + low))


def lead_two_kernel(lines, count, info, high, low, next_block, *refs):
    (*refs, next_out) = refs
    next_out[...] = next_block[...]
    blocks, (pair, send) = lead(lines, count, refs)
    for turn in range(1, high.shape[1]):

        def put(columns, total):
            send[turn - 1, :, columns] = total

        times(pair, high, low, 1, turn, put)


def lead(lines, count, refs):
    if count:
        (*refs, next_out) = refs
    outputs = refs[-2:]
    blocks, between = refs[: len(refs) - count - 2], refs[len(refs) - count - 2 : -2]
    if count:
        join_kernel(None, *between, next_out)
    fill(lines, blocks, outputs[0])
    return blocks, outputs


def lead_one_kernel(lines, count, info, high, low, pair2, *refs):
    blocks, (pair, send) = lead(lines, count, refs)
    for turn in range(1, high.shape[1]):

        def put(columns, total):
            send[turn - 1, :, columns] = total

        def add(columns, total):
            send[turn - 1, :, columns] += total

        times(pair2, high, low, 0, turn, put)
        times(pair, high, low, 1, turn, add)


def rest_one_kernel(info, high, low, pair2, pair1, *refs):
    (*from1, keep, other, total1) = refs

    def put_total(columns, total):
        total1[:, columns] = functools.reduce(jnp.add, [total] + [part[:, columns] for part in from1])

    def put_keep(columns, total):
        keep[:, columns] = total

    def add_keep(columns, total):
        keep[:, columns] += total

    times(pair2, high, low, 1, 0, put_total)
    times(pair2, high, low, 0, 0, put_keep)
    times(pair1, high, low, 1, 0, add_keep)
    for turn in range(high.shape[1]):

        def put(columns, total):
            other[turn, :, columns] = total

        times(pair1, high, low, 0, turn, put)


def both_times(info, high, low, pair, added, turn, own_put, other_put):
    first = info[0] == 0
    early = {}

    def put_early(columns, total):
        early[columns.start] = total

    def put_late(columns, total):
        late = total + added[turn, :, columns]
        own_put(columns, jnp.where(first, early[columns.start], late))
        other_put(columns, jnp.where(first, late, early[columns.start]))

    times(pair, high, low, 0, turn, put_early)
    times(pair, high, low, 1, turn, put_late)


def lead_zero_kernel(lines, info, high, low, added, *refs):
    blocks, (pair, send, cross, chip) = refs[:-4], refs[-4:]
    fill(lines, blocks, pair)
    for turn in range(1, high.shape[1]):

        def own_put(columns, total):
            send[turn - 1, :, columns] = total

        def other_put(columns, total):
            cross[turn - 1, :, columns] = total

        both_times(info, high, low, pair, added, turn, own_put, other_put)
    later = jnp.where(info[0] == 0, 1.0, 0.0)

    def put(columns, total):
        chip[:, columns] = total + later * added[0, :, columns]

    times(pair, high, low, 1 - info[0], 0, put)


def last_kernel(info, high, low, pair, added, keep):
    later = jnp.where(info[0] == 0, 0.0, 1.0)

    def put(columns, total):
        keep[:, columns] = total + later * added[0, :, columns]

    times(pair, high, low, info[0], 0, put)


def totals_kernel(info, total1, keep0, *refs):
    (*from0, own_ref, other_ref) = refs
    first = info[0] == 0
    total0 = functools.reduce(jnp.add, [keep0[...]] + [part[...] for part in from0])
    own_ref[...] = jnp.where(first, total0, total1[...])
    other_ref[...] = jnp.where(first, total1[...], total0)


def finish_kernel(spaces, info, d_keep, d_chip, next_own, next_other, *refs):
    (*parts, out_ref) = refs
    first = info[0] == 0
    (sensors, step), half = out_ref.shape, d_keep.shape[0]
    columns = pl.ds(pl.multiple_of(pl.program_id(0) * step, step), step)
    own = d_keep[:, columns] + next_own[:, columns]
    other = d_chip[:, columns] + next_other[:, columns]
    for straight, cross in zip(parts[: spaces - 1], parts[spaces - 1 :]):
        own = own + straight[:, columns]
        other = other + cross[:, columns]
    out_ref[:half, :] = jnp.where(first, own, other)
    out_ref[half:, :] = jnp.where(first, other, own)[2 * half - sensors :, :]


def on_device(model, kernels, lines, rows, spaces):
    core = lax.axis_index("core")
    info = jnp.stack([core, lax.axis_index("space"), lax.axis_index("line"), lax.axis_index("row")]).astype(jnp.int32)
    own_model = model[0]
    depth, columns = own_model.shape
    lags, sensors, width = kernels.shape
    half = -(-sensors // 32) * 16
    block = columns // spaces

    def swap(values):
        return lax.ppermute(values, "core", [(0, 1), (1, 0)])

    def onward(values):
        return lax.ppermute(values, ("line", "row"), [(i, i + 1) for i in range(lines * rows - 1)])

    def onward_across(values):
        route = [(2 * i + core, 2 * i + 3 - core) for i in range(lines * rows - 1) for core in range(2)]
        return lax.ppermute(values, ("line", "row", "core"), route)

    def over_space(sent):
        return [
            lax.ppermute(sent[d - 1], "space", [(i, (i + d) % spaces) for i in range(spaces)])
            for d in range(1, spaces)
        ]

    def over_space_and_core(sent):
        return [
            lax.ppermute(
                sent[d - 1],
                ("core", "space"),
                [(c * spaces + i, (1 - c) * spaces + (i + d) % spaces) for c in range(2) for i in range(spaces)],
            )
            for d in range(1, spaces)
        ]

    kernels_t = jnp.swapaxes(kernels, 1, 2)
    (own_t,) = call(stage_kernel, "stage", [jax.ShapeDtypeStruct(kernels_t.shape, F32)], [info, kernels_t])
    small = jax.ShapeDtypeStruct((half, 2 * width), F32)
    lag_blocks = call(spread_kernel, "spread", [small] * lags, [info, own_t, swap(kernels_t)])

    def shifted(own_block):
        held = {0: own_block, lines: own_block}
        for shift in near_first(lines)[1:]:
            step = 1 if shift <= lines - shift else -1
            held[shift] = lax.ppermute(held[shift - step], "line", [(i, (i + step) % lines) for i in range(lines)])
        moved = [held[shift] for shift in near_first(lines)[1:]]
        return [own_block], moved[:-1], moved[-1:]

    def handed(blocks):
        return [
            lax.ppermute(values, "row", [(i, (i - off) % rows) for i in range(rows)])
            for off in range(1, rows)
            for values in blocks
        ]

    between = max(lines - 2, 0)
    joint = [jax.ShapeDtypeStruct((half * between, 2 * width), F32)] * bool(between)

    pair = jax.ShapeDtypeStruct((2 * half, depth), BF16)
    one = jax.ShapeDtypeStruct((half, block), F32)
    sent = jax.ShapeDtypeStruct((spaces - 1, half, block), F32)
    whole = jax.ShapeDtypeStruct((spaces, half, block), F32)
    flops = 6 * half * depth * block

    own2, near2, far2 = shifted(lag_blocks[2])
    row2 = handed(own2)

    models = [jax.ShapeDtypeStruct((2, spaces, depth, block), BF16)] * 2
    high, low, block1, *staged = call(
        functools.partial(own_halves_kernel, lines, rows),
        "own_halves",
        models + [small] + [jax.ShapeDtypeStruct((depth, block), F32)] * spaces,
        [info, own_model, lag_blocks[1]],
    )
    joint2 = call(join_kernel, "join2", joint, [info, *near2], waits=row2) if joint else []
    high, low = call(
        other_halves_kernel,
        "other_halves",
        models,
        [info, high, low] + [swap(part) for part in staged],
        aliases={1: 0, 2: 1},
    )

    def gathered(own, near, far, row_own, near_joint):
        return own + near + far, ordered(row_own, handed(near_joint), handed(far))

    def ordered(*groups):
        each = [len(group) // (rows - 1) if rows > 1 else 0 for group in groups]
        return [
            group[off * size + at] for off in range(rows - 1) for group, size in zip(groups, each) for at in range(size)
        ]

    line2, row2 = gathered(own2, near2, far2, row2, joint2)
    own1, near1, far1 = shifted(block1)
    row_own1 = handed(own1)
    pair2, send1, *joint1, block0 = call(
        functools.partial(lead_two_kernel, lines, between),
        "lead2",
        [pair, sent] + joint + [small],
        [info, high, low, lag_blocks[0], *line2, *row2, *near1],
        waits=row_own1,
        flops=flops,
    )
    from1 = over_space(send1)
    row_near1 = handed(joint1)
    passed1 = list(call(join_kernel, "pass1", [small], [info, *far1], waits=row_near1)) if far1 else []
    line1, row1 = own1 + near1 + far1, ordered(row_own1, row_near1, handed(passed1))
    own0, near0, far0 = shifted(block0)
    pair1, send0, *joint0 = call(
        functools.partial(lead_one_kernel, lines, 1 + len(near0)),
        "lead1",
        [pair, sent, jax.ShapeDtypeStruct((half * (1 + len(near0)), 2 * width), F32)],
        [info, high, low, pair2, *line1, *row1, *own0, *near0],
        waits=from1,
        flops=2 * flops,
    )
    from0 = over_space(send0)
    line0, row0 = gathered(own0, near0, far0, [], joint0)
    keep0, early1, total1 = call(
        rest_one_kernel,
        "rest1",
        [one, whole, one],
        [info, high, low, pair2, pair1, *from1],
        waits=row0[:1],
        flops=3 * flops,
    )
    pair0, d_send, d_cross, d_chip = call(
        functools.partial(lead_zero_kernel, lines),
        "lead0",
        [pair, sent, sent, one],
        [info, high, low, early1, *line0, *row0],
        flops=3 * flops,
    )
    d_from, d_from_cross = over_space(d_send), over_space_and_core(d_cross)
    next_same, next_cross = call(totals_kernel, "totals", [one, one], [info, total1, keep0, *from0], waits=row0[-1:])
    (d_keep,) = call(last_kernel, "last", [one], [info, high, low, pair0, early1], flops=flops)
    operands = [d_keep, swap(d_chip), onward(next_same), onward_across(next_cross), *d_from, *d_from_cross]
    step = block if block % 128 else 128
    result = pl.pallas_call(
        functools.partial(finish_kernel, spaces),
        grid=(block // step,),
        out_shape=jax.ShapeDtypeStruct((sensors, block), F32),
        in_specs=[SMEM_SPEC] + [VMEM_SPEC] * len(operands),
        out_specs=pl.BlockSpec((sensors, step), lambda at: (0, at)),
        compiler_params=pltpu.CompilerParams(vmem_limit_bytes=VMEM_LIMIT),
        name="finish",
    )(info, *operands)
    return result[None]


def solution(mesh):
    chips, spaces = mesh.shape["tm"] // 2, mesh.shape["space"]
    rows = 1 if chips % 2 else 2
    lines = chips // rows
    grid = Mesh(mesh.devices.reshape(lines, rows, 2, spaces), ("line", "row", "core", "space"))
    return jax.shard_map(
        functools.partial(on_device, lines=lines, rows=rows, spaces=spaces),
        mesh=grid,
        in_specs=(P(("line", "row", "core"), "space", None), P(None, None, ("space", "line", "row", "core"))),
        out_specs=P(("line", "row", "core"), None, "space"),
        check_vma=False,
    )
```

```python
import functools

import jax
import jax.numpy as jnp
from jax import lax
from jax.experimental import pallas as pl
from jax.experimental.pallas import tpu as pltpu
from jax.sharding import Mesh, PartitionSpec as P

F32, BF16 = jnp.float32, jnp.bfloat16
VMEM_LIMIT = 28 * 2**20
SMEM_SPEC = pl.BlockSpec(memory_space=pltpu.SMEM)
VMEM_SPEC = pl.BlockSpec(memory_space=pltpu.VMEM)


def split(values):
    high = values.astype(BF16)
    return high, (values - high.astype(F32)).astype(BF16)


def call(kernel, name, shapes, operands, waits=(), flops=0, aliases=None):
    def body(*refs):
        kernel(*refs[: len(operands)], *refs[len(operands) + len(waits) :])

    return pl.pallas_call(
        body,
        out_shape=shapes,
        in_specs=[SMEM_SPEC] + [VMEM_SPEC] * (len(operands) - 1) + [pl.BlockSpec(memory_space=pl.ANY)] * len(waits),
        out_specs=[VMEM_SPEC] * len(shapes),
        input_output_aliases=aliases or {},
        compiler_params=pltpu.CompilerParams(vmem_limit_bytes=VMEM_LIMIT),
        cost_estimate=pl.CostEstimate(flops=flops, bytes_accessed=1, transcendentals=0),
        name=name,
    )(*operands, *waits)


def stage_kernel(info, source_ref, out_ref):
    out_ref[...] = source_ref[...]


def spread_kernel(info, own_ref, other_ref, *lag_refs):
    first = info[0] == 0
    half = lag_refs[0].shape[0]
    sensors = own_ref.shape[2]
    for lag, out_ref in enumerate(lag_refs):
        own, other = own_ref[lag], other_ref[lag]
        both = jnp.concatenate([jnp.where(first, own, other), jnp.where(first, other, own)], axis=0).T
        out_ref[...] = jnp.where(first, both[:half], both[sensors - half :])


def own_halves_kernel(lines, rows, info, model_ref, next_ref, high_ref, low_ref, next_out, *staged_refs):
    next_out[...] = next_ref[...]
    spaces, depth, block = high_ref.shape[1:]
    width = depth // (lines * rows)
    for turn, staged_ref in enumerate(staged_refs):
        columns = pl.ds(pl.multiple_of(lax.rem(info[1] + turn, spaces) * block, block), block)
        for at in range(lines * rows):
            source = pl.ds(pl.multiple_of(chip_at(at, info, lines, rows) * width, width), width)
            target = slice(at * width, (at + 1) * width)
            values = model_ref[source, columns]
            staged_ref[target, :] = values
            high_ref[info[0], turn, target], low_ref[info[0], turn, target] = split(values)


def other_halves_kernel(info, high_in, low_in, *refs):
    (*staged_refs, high_ref, low_ref) = refs
    for turn, staged_ref in enumerate(staged_refs):
        high_ref[1 - info[0], turn], low_ref[1 - info[0], turn] = split(staged_ref[...])


def near_first(lines):
    return [0] + sorted(range(1, lines), key=lambda shift: (min(shift, lines - shift), shift))


def chip_at(at, info, lines, rows):
    row_off, shift = at // lines, at % lines
    return lax.rem(info[2] - shift + lines, lines) * rows + lax.rem(info[3] + row_off, rows)


def fill(lines, blocks, pair_ref):
    half, width = pair_ref.shape[0] // 2, blocks[0].shape[1]
    count = 0
    for block in blocks:
        for start in range(0, block.shape[0], half):
            at = count // lines * lines + near_first(lines)[count % lines]
            columns = slice(at * width, (at + 1) * width)
            pair_ref[:half, columns], pair_ref[half:, columns] = split(block[start : start + half])
            count += 1


def join_kernel(info, *refs):
    (*parts, out_ref) = refs
    start = 0
    for part in parts:
        out_ref[start : start + part.shape[0]] = part[...]
        start += part.shape[0]


def times(pair_ref, high_ref, low_ref, slot, turn, put):
    half = pair_ref.shape[0] // 2
    width = high_ref.shape[3]
    step = width if width % 256 else 256
    for start in range(0, width, step):
        columns = slice(start, start + step)
        both = jnp.dot(pair_ref[...], high_ref[slot, turn, :, columns], preferred_element_type=F32)
        low = jnp.dot(pair_ref[:half], low_ref[slot, turn, :, columns], preferred_element_type=F32)
        put(columns, both[:half] + (both[half:] + low))


def lead_two_kernel(lines, count, info, high, low, next_block, *refs):
    (*refs, next_out) = refs
    next_out[...] = next_block[...]
    blocks, (pair, send) = lead(lines, count, refs)
    for turn in range(1, high.shape[1]):

        def put(columns, total):
            send[turn - 1, :, columns] = total

        times(pair, high, low, 1, turn, put)


def lead(lines, count, refs):
    if count:
        (*refs, next_out) = refs
    outputs = refs[-2:]
    blocks, between = refs[: len(refs) - count - 2], refs[len(refs) - count - 2 : -2]
    if count:
        join_kernel(None, *between, next_out)
    fill(lines, blocks, outputs[0])
    return blocks, outputs


def lead_one_kernel(lines, count, info, high, low, pair2, *refs):
    blocks, (pair, send) = lead(lines, count, refs)
    for turn in range(1, high.shape[1]):

        def put(columns, total):
            send[turn - 1, :, columns] = total

        def add(columns, total):
            send[turn - 1, :, columns] += total

        times(pair2, high, low, 0, turn, put)
        times(pair, high, low, 1, turn, add)


def rest_one_kernel(info, high, low, pair2, pair1, *refs):
    (*from1, keep, other, total1) = refs

    def put_total(columns, total):
        total1[:, columns] = functools.reduce(jnp.add, [total] + [part[:, columns] for part in from1])

    def put_keep(columns, total):
        keep[:, columns] = total

    def add_keep(columns, total):
        keep[:, columns] += total

    times(pair2, high, low, 1, 0, put_total)
    times(pair2, high, low, 0, 0, put_keep)
    times(pair1, high, low, 1, 0, add_keep)
    for turn in range(high.shape[1]):

        def put(columns, total):
            other[turn, :, columns] = total

        times(pair1, high, low, 0, turn, put)


def both_times(info, high, low, pair, added, turn, own_put, other_put):
    first = info[0] == 0
    early = {}

    def put_early(columns, total):
        early[columns.start] = total

    def put_late(columns, total):
        late = total + added[turn, :, columns]
        own_put(columns, jnp.where(first, early[columns.start], late))
        other_put(columns, jnp.where(first, late, early[columns.start]))

    times(pair, high, low, 0, turn, put_early)
    times(pair, high, low, 1, turn, put_late)


def lead_zero_kernel(lines, info, high, low, added, *refs):
    blocks, (pair, send, cross, chip) = refs[:-4], refs[-4:]
    fill(lines, blocks, pair)
    for turn in range(1, high.shape[1]):

        def own_put(columns, total):
            send[turn - 1, :, columns] = total

        def other_put(columns, total):
            cross[turn - 1, :, columns] = total

        both_times(info, high, low, pair, added, turn, own_put, other_put)
    later = jnp.where(info[0] == 0, 1.0, 0.0)

    def put(columns, total):
        chip[:, columns] = total + later * added[0, :, columns]

    times(pair, high, low, 1 - info[0], 0, put)


def last_kernel(info, high, low, pair, added, keep):
    later = jnp.where(info[0] == 0, 0.0, 1.0)

    def put(columns, total):
        keep[:, columns] = total + later * added[0, :, columns]

    times(pair, high, low, info[0], 0, put)


def totals_kernel(info, total1, keep0, *refs):
    (*from0, own_ref, other_ref) = refs
    first = info[0] == 0
    total0 = functools.reduce(jnp.add, [keep0[...]] + [part[...] for part in from0])
    own_ref[...] = jnp.where(first, total0, total1[...])
    other_ref[...] = jnp.where(first, total1[...], total0)


def add_kernel(info, *refs):
    count = len(refs) // 2 - 1
    for terms, out_ref in ((refs[:count], refs[-2]), (refs[count:-2], refs[-1])):
        out_ref[...] = functools.reduce(jnp.add, [term[...] for term in terms])


def finish_kernel(info, own_sum, other_sum, next_own, next_other, out_ref):
    first = info[0] == 0
    sensors, half = out_ref.shape[0], own_sum.shape[0]
    own = own_sum[...] + next_own[...]
    other = other_sum[...] + next_other[...]
    out_ref[:half, :] = jnp.where(first, own, other)
    out_ref[half:, :] = jnp.where(first, other, own)[2 * half - sensors :, :]


def on_device(model, kernels, lines, rows, spaces):
    core = lax.axis_index("core")
    info = jnp.stack([core, lax.axis_index("space"), lax.axis_index("line"), lax.axis_index("row")]).astype(jnp.int32)
    own_model = model[0]
    depth, columns = own_model.shape
    lags, sensors, width = kernels.shape
    half = -(-sensors // 32) * 16
    block = columns // spaces

    def swap(values):
        return lax.ppermute(values, "core", [(0, 1), (1, 0)])

    def onward(values):
        return lax.ppermute(values, ("line", "row"), [(i, i + 1) for i in range(lines * rows - 1)])

    def onward_across(values):
        route = [(2 * i + core, 2 * i + 3 - core) for i in range(lines * rows - 1) for core in range(2)]
        return lax.ppermute(values, ("line", "row", "core"), route)

    def over_space(sent):
        return [
            lax.ppermute(sent[d - 1], "space", [(i, (i + d) % spaces) for i in range(spaces)])
            for d in range(1, spaces)
        ]

    def over_space_and_core(sent):
        return [
            lax.ppermute(
                sent[d - 1],
                ("core", "space"),
                [(c * spaces + i, (1 - c) * spaces + (i + d) % spaces) for c in range(2) for i in range(spaces)],
            )
            for d in range(1, spaces)
        ]

    kernels_t = jnp.swapaxes(kernels, 1, 2)
    (own_t,) = call(stage_kernel, "stage", [jax.ShapeDtypeStruct(kernels_t.shape, F32)], [info, kernels_t])
    small = jax.ShapeDtypeStruct((half, 2 * width), F32)
    lag_blocks = call(spread_kernel, "spread", [small] * lags, [info, own_t, swap(kernels_t)])

    def shifted(own_block):
        held = {0: own_block, lines: own_block}
        for shift in near_first(lines)[1:]:
            step = 1 if shift <= lines - shift else -1
            held[shift] = lax.ppermute(held[shift - step], "line", [(i, (i + step) % lines) for i in range(lines)])
        moved = [held[shift] for shift in near_first(lines)[1:]]
        return [own_block], moved[:-1], moved[-1:]

    def handed(blocks):
        return [
            lax.ppermute(values, "row", [(i, (i - off) % rows) for i in range(rows)])
            for off in range(1, rows)
            for values in blocks
        ]

    between = max(lines - 2, 0)
    joint = [jax.ShapeDtypeStruct((half * between, 2 * width), F32)] * bool(between)

    pair = jax.ShapeDtypeStruct((2 * half, depth), BF16)
    one = jax.ShapeDtypeStruct((half, block), F32)
    sent = jax.ShapeDtypeStruct((spaces - 1, half, block), F32)
    whole = jax.ShapeDtypeStruct((spaces, half, block), F32)
    flops = 6 * half * depth * block

    own2, near2, far2 = shifted(lag_blocks[2])
    row2 = handed(own2)

    models = [jax.ShapeDtypeStruct((2, spaces, depth, block), BF16)] * 2
    high, low, block1, *staged = call(
        functools.partial(own_halves_kernel, lines, rows),
        "own_halves",
        models + [small] + [jax.ShapeDtypeStruct((depth, block), F32)] * spaces,
        [info, own_model, lag_blocks[1]],
    )
    joint2 = call(join_kernel, "join2", joint, [info, *near2], waits=row2) if joint else []
    high, low = call(
        other_halves_kernel,
        "other_halves",
        models,
        [info, high, low] + [swap(part) for part in staged],
        aliases={1: 0, 2: 1},
    )

    def gathered(own, near, far, row_own, near_joint):
        return own + near + far, ordered(row_own, handed(near_joint), handed(far))

    def ordered(*groups):
        each = [len(group) // (rows - 1) if rows > 1 else 0 for group in groups]
        return [
            group[off * size + at] for off in range(rows - 1) for group, size in zip(groups, each) for at in range(size)
        ]

    line2, row2 = gathered(own2, near2, far2, row2, joint2)
    own1, near1, far1 = shifted(block1)
    row_own1 = handed(own1)
    pair2, send1, *joint1, block0 = call(
        functools.partial(lead_two_kernel, lines, between),
        "lead2",
        [pair, sent] + joint + [small],
        [info, high, low, lag_blocks[0], *line2, *row2, *near1],
        waits=row_own1 + far1,
        flops=flops,
    )
    from1 = over_space(send1)
    line1, row1 = gathered(own1, near1, far1, row_own1, joint1)
    own0, near0, far0 = shifted(block0)
    pair1, send0, *joint0 = call(
        functools.partial(lead_one_kernel, lines, 1 + len(near0)),
        "lead1",
        [pair, sent, jax.ShapeDtypeStruct((half * (1 + len(near0)), 2 * width), F32)],
        [info, high, low, pair2, *line1, *row1, *own0, *near0],
        waits=from1,
        flops=2 * flops,
    )
    from0 = over_space(send0)
    keep0, early1, total1 = call(
        rest_one_kernel,
        "rest1",
        [one, whole, one],
        [info, high, low, pair2, pair1, *from1],
        flops=3 * flops,
    )
    passed0 = list(call(join_kernel, "pass0", [small], [info, *far0], waits=[early1])) if far0 else []
    line0, row0 = own0 + near0 + far0, ordered(handed(joint0), handed(passed0))
    pair0, d_send, d_cross, d_chip = call(
        functools.partial(lead_zero_kernel, lines),
        "lead0",
        [pair, sent, sent, one],
        [info, high, low, early1, *line0, *row0],
        flops=3 * flops,
    )
    d_from, d_from_cross = over_space(d_send), over_space_and_core(d_cross)
    next_same, next_cross = call(totals_kernel, "totals", [one, one], [info, total1, keep0, *from0], waits=row0[-1:])
    (d_keep,) = call(last_kernel, "last", [one], [info, high, low, pair0, early1], flops=flops)
    sums = call(add_kernel, "add", [one, one], [info, d_keep, *d_from, swap(d_chip), *d_from_cross])
    (result,) = call(
        finish_kernel,
        "finish",
        [jax.ShapeDtypeStruct((sensors, block), F32)],
        [info, *sums, onward(next_same), onward_across(next_cross)],
    )
    return result[None]


def solution(mesh):
    chips, spaces = mesh.shape["tm"] // 2, mesh.shape["space"]
    rows = 1 if chips % 2 else 2
    lines = chips // rows
    grid = Mesh(mesh.devices.reshape(lines, rows, 2, spaces), ("line", "row", "core", "space"))
    return jax.shard_map(
        functools.partial(on_device, lines=lines, rows=rows, spaces=spaces),
        mesh=grid,
        in_specs=(P(("line", "row", "core"), "space", None), P(None, None, ("space", "line", "row", "core"))),
        out_specs=P(("line", "row", "core"), None, "space"),
        check_vma=False,
    )
```

```python
import functools

import jax
import jax.numpy as jnp
from jax import lax
from jax.experimental import pallas as pl
from jax.experimental.pallas import tpu as pltpu
from jax.sharding import Mesh, PartitionSpec as P

F32, BF16 = jnp.float32, jnp.bfloat16
VMEM_LIMIT = 28 * 2**20
SMEM_SPEC = pl.BlockSpec(memory_space=pltpu.SMEM)
VMEM_SPEC = pl.BlockSpec(memory_space=pltpu.VMEM)


def split(values):
    high = values.astype(BF16)
    return high, (values - high.astype(F32)).astype(BF16)


def call(kernel, name, shapes, operands, waits=(), flops=0, aliases=None):
    def body(*refs):
        kernel(*refs[: len(operands)], *refs[len(operands) + len(waits) :])

    return pl.pallas_call(
        body,
        out_shape=shapes,
        in_specs=[SMEM_SPEC] + [VMEM_SPEC] * (len(operands) - 1) + [pl.BlockSpec(memory_space=pl.ANY)] * len(waits),
        out_specs=[VMEM_SPEC] * len(shapes),
        input_output_aliases=aliases or {},
        compiler_params=pltpu.CompilerParams(vmem_limit_bytes=VMEM_LIMIT),
        cost_estimate=pl.CostEstimate(flops=flops, bytes_accessed=1, transcendentals=0),
        name=name,
    )(*operands, *waits)


def stage_kernel(info, source_ref, out_ref):
    out_ref[...] = source_ref[...]


def spread_kernel(info, own_ref, other_ref, *lag_refs):
    first = info[0] == 0
    half = lag_refs[0].shape[0]
    sensors = own_ref.shape[2]
    for lag, out_ref in enumerate(lag_refs):
        own, other = own_ref[lag], other_ref[lag]
        both = jnp.concatenate([jnp.where(first, own, other), jnp.where(first, other, own)], axis=0).T
        out_ref[...] = jnp.where(first, both[:half], both[sensors - half :])


def own_halves_kernel(lines, rows, info, model_ref, next_ref, high_ref, low_ref, next_out, *staged_refs):
    next_out[...] = next_ref[...]
    spaces, depth, block = high_ref.shape[1:]
    width = depth // (lines * rows)
    for turn, staged_ref in enumerate(staged_refs):
        columns = pl.ds(pl.multiple_of(lax.rem(info[1] + turn, spaces) * block, block), block)
        for at in range(lines * rows):
            source = pl.ds(pl.multiple_of(chip_at(at, info, lines, rows) * width, width), width)
            target = slice(at * width, (at + 1) * width)
            values = model_ref[source, columns]
            staged_ref[target, :] = values
            high_ref[info[0], turn, target], low_ref[info[0], turn, target] = split(values)


def other_halves_kernel(info, high_in, low_in, *refs):
    (*staged_refs, high_ref, low_ref) = refs
    for turn, staged_ref in enumerate(staged_refs):
        high_ref[1 - info[0], turn], low_ref[1 - info[0], turn] = split(staged_ref[...])


def near_first(lines):
    return [0] + sorted(range(1, lines), key=lambda shift: (min(shift, lines - shift), shift))


def chip_at(at, info, lines, rows):
    row_off, shift = at // lines, at % lines
    return lax.rem(info[2] - shift + lines, lines) * rows + lax.rem(info[3] + row_off, rows)


def fill(lines, blocks, pair_ref):
    half, width = pair_ref.shape[0] // 2, blocks[0].shape[1]
    count = 0
    for block in blocks:
        for start in range(0, block.shape[0], half):
            at = count // lines * lines + near_first(lines)[count % lines]
            columns = slice(at * width, (at + 1) * width)
            pair_ref[:half, columns], pair_ref[half:, columns] = split(block[start : start + half])
            count += 1


def join_kernel(info, *refs):
    (*parts, out_ref) = refs
    start = 0
    for part in parts:
        out_ref[start : start + part.shape[0]] = part[...]
        start += part.shape[0]


def times(pair_ref, high_ref, low_ref, slot, turn, put):
    half = pair_ref.shape[0] // 2
    width = high_ref.shape[3]
    step = width if width % 256 else 256
    for start in range(0, width, step):
        columns = slice(start, start + step)
        both = jnp.dot(pair_ref[...], high_ref[slot, turn, :, columns], preferred_element_type=F32)
        low = jnp.dot(pair_ref[:half], low_ref[slot, turn, :, columns], preferred_element_type=F32)
        put(columns, both[:half] + (both[half:] + low))


def lead_two_kernel(lines, count, info, high, low, next_block, *refs):
    (*refs, next_out) = refs
    next_out[...] = next_block[...]
    blocks, (pair, send) = lead(lines, count, refs)
    for turn in range(1, high.shape[1]):

        def put(columns, total):
            send[turn - 1, :, columns] = total

        times(pair, high, low, 1, turn, put)


def lead(lines, count, refs):
    if count:
        (*refs, next_out) = refs
    outputs = refs[-2:]
    blocks, between = refs[: len(refs) - count - 2], refs[len(refs) - count - 2 : -2]
    if count:
        join_kernel(None, *between, next_out)
    fill(lines, blocks, outputs[0])
    return blocks, outputs


def lead_one_kernel(lines, count, info, high, low, pair2, *refs):
    blocks, (pair, send) = lead(lines, count, refs)
    for turn in range(1, high.shape[1]):

        def put(columns, total):
            send[turn - 1, :, columns] = total

        def add(columns, total):
            send[turn - 1, :, columns] += total

        times(pair2, high, low, 0, turn, put)
        times(pair, high, low, 1, turn, add)


def rest_one_kernel(info, high, low, pair2, pair1, *refs):
    (*from1, keep, other, total1) = refs

    def put_total(columns, total):
        total1[:, columns] = functools.reduce(jnp.add, [total] + [part[:, columns] for part in from1])

    def put_keep(columns, total):
        keep[:, columns] = total

    def add_keep(columns, total):
        keep[:, columns] += total

    times(pair2, high, low, 1, 0, put_total)
    times(pair2, high, low, 0, 0, put_keep)
    times(pair1, high, low, 1, 0, add_keep)
    for turn in range(high.shape[1]):

        def put(columns, total):
            other[turn, :, columns] = total

        times(pair1, high, low, 0, turn, put)


def both_times(info, high, low, pair, added, turn, own_put, other_put):
    first = info[0] == 0
    early = {}

    def put_early(columns, total):
        early[columns.start] = total

    def put_late(columns, total):
        late = total + added[turn, :, columns]
        own_put(columns, jnp.where(first, early[columns.start], late))
        other_put(columns, jnp.where(first, late, early[columns.start]))

    times(pair, high, low, 0, turn, put_early)
    times(pair, high, low, 1, turn, put_late)


def lead_zero_kernel(lines, info, high, low, added, *refs):
    blocks, (pair, send, cross, chip) = refs[:-4], refs[-4:]
    fill(lines, blocks, pair)
    for turn in range(1, high.shape[1]):

        def own_put(columns, total):
            send[turn - 1, :, columns] = total

        def other_put(columns, total):
            cross[turn - 1, :, columns] = total

        both_times(info, high, low, pair, added, turn, own_put, other_put)
    later = jnp.where(info[0] == 0, 1.0, 0.0)

    def put(columns, total):
        chip[:, columns] = total + later * added[0, :, columns]

    times(pair, high, low, 1 - info[0], 0, put)


def last_kernel(info, high, low, pair, added, keep):
    later = jnp.where(info[0] == 0, 0.0, 1.0)

    def put(columns, total):
        keep[:, columns] = total + later * added[0, :, columns]

    times(pair, high, low, info[0], 0, put)


def total_kernel(info, *refs):
    refs[-1][...] = functools.reduce(jnp.add, [term[...] for term in refs[:-1]])


def pass_kernel(info, *refs):
    count = len(refs) // 2
    for source, target in zip(refs[:count], refs[count:]):
        target[...] = source[...]


def add_kernel(info, *refs):
    count = len(refs) // 2 - 1
    for terms, out_ref in ((refs[:count], refs[-2]), (refs[count:-2], refs[-1])):
        out_ref[...] = functools.reduce(jnp.add, [term[...] for term in terms])


def finish_kernel(info, own_sum, other_sum, next_own, next_other, out_ref):
    first = info[0] == 0
    sensors, half = out_ref.shape[0], own_sum.shape[0]
    own = own_sum[...] + next_own[...]
    other = other_sum[...] + next_other[...]
    out_ref[:half, :] = jnp.where(first, own, other)
    out_ref[half:, :] = jnp.where(first, other, own)[2 * half - sensors :, :]


def on_device(model, kernels, lines, rows, spaces):
    core = lax.axis_index("core")
    info = jnp.stack([core, lax.axis_index("space"), lax.axis_index("line"), lax.axis_index("row")]).astype(jnp.int32)
    own_model = model[0]
    depth, columns = own_model.shape
    lags, sensors, width = kernels.shape
    half = -(-sensors // 32) * 16
    block = columns // spaces

    def swap(values):
        return lax.ppermute(values, "core", [(0, 1), (1, 0)])

    def onward(values, target):
        def from_core(source):
            route = [(2 * i + source, 2 * i + 2 + target) for i in range(lines * rows - 1)]
            return lax.ppermute(values, ("line", "row", "core"), route)

        return from_core(target), from_core(1 - target)

    def over_space(sent):
        return [
            lax.ppermute(sent[d - 1], "space", [(i, (i + d) % spaces) for i in range(spaces)])
            for d in range(1, spaces)
        ]

    def over_space_and_core(sent):
        return [
            lax.ppermute(
                sent[d - 1],
                ("core", "space"),
                [(c * spaces + i, (1 - c) * spaces + (i + d) % spaces) for c in range(2) for i in range(spaces)],
            )
            for d in range(1, spaces)
        ]

    kernels_t = jnp.swapaxes(kernels, 1, 2)
    (own_t,) = call(stage_kernel, "stage", [jax.ShapeDtypeStruct(kernels_t.shape, F32)], [info, kernels_t])
    small = jax.ShapeDtypeStruct((half, 2 * width), F32)
    lag_blocks = call(spread_kernel, "spread", [small] * lags, [info, own_t, swap(kernels_t)])

    def shifted(own_block):
        held = {0: own_block, lines: own_block}
        for shift in near_first(lines)[1:]:
            step = 1 if shift <= lines - shift else -1
            held[shift] = lax.ppermute(held[shift - step], "line", [(i, (i + step) % lines) for i in range(lines)])
        moved = [held[shift] for shift in near_first(lines)[1:]]
        return [own_block], moved[:-1], moved[-1:]

    def handed(blocks):
        return [
            lax.ppermute(values, "row", [(i, (i - off) % rows) for i in range(rows)])
            for off in range(1, rows)
            for values in blocks
        ]

    between = max(lines - 2, 0)
    joint = [jax.ShapeDtypeStruct((half * between, 2 * width), F32)] * bool(between)

    pair = jax.ShapeDtypeStruct((2 * half, depth), BF16)
    one = jax.ShapeDtypeStruct((half, block), F32)
    sent = jax.ShapeDtypeStruct((spaces - 1, half, block), F32)
    whole = jax.ShapeDtypeStruct((spaces, half, block), F32)
    flops = 6 * half * depth * block

    own2, near2, far2 = shifted(lag_blocks[2])
    row2 = handed(own2)

    models = [jax.ShapeDtypeStruct((2, spaces, depth, block), BF16)] * 2
    high, low, block1, *staged = call(
        functools.partial(own_halves_kernel, lines, rows),
        "own_halves",
        models + [small] + [jax.ShapeDtypeStruct((depth, block), F32)] * spaces,
        [info, own_model, lag_blocks[1]],
    )
    joint2 = call(join_kernel, "join2", joint, [info, *near2], waits=row2) if joint else []
    high, low = call(
        other_halves_kernel,
        "other_halves",
        models,
        [info, high, low] + [swap(part) for part in staged],
        aliases={1: 0, 2: 1},
    )

    def gathered(own, near, far, row_own, near_joint):
        return own + near + far, ordered(row_own, handed(near_joint), handed(far))

    def ordered(*groups):
        each = [len(group) // (rows - 1) if rows > 1 else 0 for group in groups]
        return [
            group[off * size + at] for off in range(rows - 1) for group, size in zip(groups, each) for at in range(size)
        ]

    line2, row2 = gathered(own2, near2, far2, row2, joint2)
    own1, near1, far1 = shifted(block1)
    row_own1 = handed(own1)
    pair2, send1, *joint1, block0 = call(
        functools.partial(lead_two_kernel, lines, between),
        "lead2",
        [pair, sent] + joint + [small],
        [info, high, low, lag_blocks[0], *line2, *row2, *near1],
        waits=row_own1 + far1,
        flops=flops,
    )
    from1 = over_space(send1)
    line1, row1 = gathered(own1, near1, far1, row_own1, joint1)
    own0, near0, far0 = shifted(block0)
    pair1, send0, *joint0 = call(
        functools.partial(lead_one_kernel, lines, 1 + len(near0)),
        "lead1",
        [pair, sent, jax.ShapeDtypeStruct((half * (1 + len(near0)), 2 * width), F32)],
        [info, high, low, pair2, *line1, *row1, *own0, *near0],
        waits=from1,
        flops=2 * flops,
    )
    from0 = over_space(send0)
    keep0, early1, total1 = call(
        rest_one_kernel,
        "rest1",
        [one, whole, one],
        [info, high, low, pair2, pair1, *from1],
        waits=far0,
        flops=3 * flops,
    )
    line0, row0 = gathered(own0, near0, far0, [], joint0)
    pair0, d_send, d_cross, d_chip = call(
        functools.partial(lead_zero_kernel, lines),
        "lead0",
        [pair, sent, sent, one],
        [info, high, low, early1, *line0, *row0],
        flops=3 * flops,
    )
    d_from, d_from_cross = over_space(d_send), over_space_and_core(d_cross)
    (total0,) = call(total_kernel, "total0", [one], [info, keep0, *from0], waits=row0[-1:])
    (passed1,) = call(pass_kernel, "pass1", [one], [info, total1], waits=row0)
    same1, cross1 = onward(passed1, 1)
    same0, cross0 = onward(total0, 0)
    (d_keep,) = call(last_kernel, "last", [one], [info, high, low, pair0, early1], flops=flops)
    sums = call(
        add_kernel, "add", [one, one], [info, d_keep, same1, *d_from, swap(d_chip), cross1, *d_from_cross]
    )
    (result,) = call(
        finish_kernel,
        "finish",
        [jax.ShapeDtypeStruct((sensors, block), F32)],
        [info, *sums, same0, cross0],
    )
    return result[None]


def solution(mesh):
    chips, spaces = mesh.shape["tm"] // 2, mesh.shape["space"]
    rows = 1 if chips % 2 else 2
    lines = chips // rows
    grid = Mesh(mesh.devices.reshape(lines, rows, 2, spaces), ("line", "row", "core", "space"))
    return jax.shard_map(
        functools.partial(on_device, lines=lines, rows=rows, spaces=spaces),
        mesh=grid,
        in_specs=(P(("line", "row", "core"), "space", None), P(None, None, ("space", "line", "row", "core"))),
        out_specs=P(("line", "row", "core"), None, "space"),
        check_vma=False,
    )
```

```python
import functools

import jax
import jax.numpy as jnp
from jax import lax
from jax.experimental import pallas as pl
from jax.experimental.pallas import tpu as pltpu
from jax.sharding import Mesh, PartitionSpec as P

F32, BF16 = jnp.float32, jnp.bfloat16
VMEM_LIMIT = 28 * 2**20
SMEM_SPEC = pl.BlockSpec(memory_space=pltpu.SMEM)
VMEM_SPEC = pl.BlockSpec(memory_space=pltpu.VMEM)


def split(values):
    high = values.astype(BF16)
    return high, (values - high.astype(F32)).astype(BF16)


def call(kernel, name, shapes, operands, waits=(), flops=0, aliases=None):
    def body(*refs):
        kernel(*refs[: len(operands)], *refs[len(operands) + len(waits) :])

    return pl.pallas_call(
        body,
        out_shape=shapes,
        in_specs=[SMEM_SPEC] + [VMEM_SPEC] * (len(operands) - 1) + [pl.BlockSpec(memory_space=pl.ANY)] * len(waits),
        out_specs=[VMEM_SPEC] * len(shapes),
        input_output_aliases=aliases or {},
        compiler_params=pltpu.CompilerParams(vmem_limit_bytes=VMEM_LIMIT),
        cost_estimate=pl.CostEstimate(flops=flops, bytes_accessed=1, transcendentals=0),
        name=name,
    )(*operands, *waits)


def stage_kernel(info, source_ref, out_ref):
    out_ref[...] = source_ref[...]


def spread_kernel(info, own_ref, other_ref, *lag_refs):
    first = info[0] == 0
    half = lag_refs[0].shape[0]
    sensors = own_ref.shape[2]
    for lag, out_ref in enumerate(lag_refs):
        own, other = own_ref[lag], other_ref[lag]
        both = jnp.concatenate([jnp.where(first, own, other), jnp.where(first, other, own)], axis=0).T
        out_ref[...] = jnp.where(first, both[:half], both[sensors - half :])


def own_halves_kernel(lines, rows, info, model_ref, next_ref, high_ref, low_ref, next_out, *staged_refs):
    next_out[...] = next_ref[...]
    spaces, depth, block = high_ref.shape[1:]
    width = depth // (lines * rows)
    for turn, staged_ref in enumerate(staged_refs):
        columns = pl.ds(pl.multiple_of(lax.rem(info[1] + turn, spaces) * block, block), block)
        for at in range(lines * rows):
            source = pl.ds(pl.multiple_of(chip_at(at, info, lines, rows) * width, width), width)
            target = slice(at * width, (at + 1) * width)
            values = model_ref[source, columns]
            staged_ref[target, :] = values
            high_ref[info[0], turn, target], low_ref[info[0], turn, target] = split(values)


def other_halves_kernel(info, high_in, low_in, *refs):
    (*staged_refs, high_ref, low_ref) = refs
    for turn, staged_ref in enumerate(staged_refs):
        high_ref[1 - info[0], turn], low_ref[1 - info[0], turn] = split(staged_ref[...])


def near_first(lines):
    return [0] + sorted(range(1, lines), key=lambda shift: (min(shift, lines - shift), shift))


def chip_at(at, info, lines, rows):
    row_off, shift = at // lines, at % lines
    return lax.rem(info[2] - shift + lines, lines) * rows + lax.rem(info[3] + row_off, rows)


def fill(lines, blocks, pair_ref):
    half, width = pair_ref.shape[0] // 2, blocks[0].shape[1]
    count = 0
    for block in blocks:
        for start in range(0, block.shape[0], half):
            at = count // lines * lines + near_first(lines)[count % lines]
            columns = slice(at * width, (at + 1) * width)
            pair_ref[:half, columns], pair_ref[half:, columns] = split(block[start : start + half])
            count += 1


def join_kernel(info, *refs):
    (*parts, out_ref) = refs
    start = 0
    for part in parts:
        out_ref[start : start + part.shape[0]] = part[...]
        start += part.shape[0]


def times(pair_ref, high_ref, low_ref, slot, turn, put):
    half = pair_ref.shape[0] // 2
    width = high_ref.shape[3]
    step = width if width % 256 else 256
    for start in range(0, width, step):
        columns = slice(start, start + step)
        both = jnp.dot(pair_ref[...], high_ref[slot, turn, :, columns], preferred_element_type=F32)
        low = jnp.dot(pair_ref[:half], low_ref[slot, turn, :, columns], preferred_element_type=F32)
        put(columns, both[:half] + (both[half:] + low))


def lead_two_kernel(lines, count, info, high, low, next_block, *refs):
    (*refs, next_out) = refs
    next_out[...] = next_block[...]
    blocks, (pair, send) = lead(lines, count, refs)
    for turn in range(1, high.shape[1]):

        def put(columns, total):
            send[turn - 1, :, columns] = total

        times(pair, high, low, 1, turn, put)


def lead(lines, count, refs):
    if count:
        (*refs, next_out) = refs
    outputs = refs[-2:]
    blocks, between = refs[: len(refs) - count - 2], refs[len(refs) - count - 2 : -2]
    if count:
        join_kernel(None, *between, next_out)
    fill(lines, blocks, outputs[0])
    return blocks, outputs


def lead_one_kernel(lines, count, info, high, low, pair2, *refs):
    blocks, (pair, send) = lead(lines, count, refs)
    for turn in range(1, high.shape[1]):

        def put(columns, total):
            send[turn - 1, :, columns] = total

        def add(columns, total):
            send[turn - 1, :, columns] += total

        times(pair2, high, low, 0, turn, put)
        times(pair, high, low, 1, turn, add)


def rest_one_kernel(info, high, low, pair2, pair1, *refs):
    (*from1, other, total1) = refs

    def put_total(columns, total):
        total1[:, columns] = functools.reduce(jnp.add, [total] + [part[:, columns] for part in from1])

    times(pair2, high, low, 1, 0, put_total)
    for turn in range(high.shape[1]):

        def put(columns, total):
            other[turn, :, columns] = total

        times(pair1, high, low, 0, turn, put)


def both_times(info, high, low, pair, added, turn, own_put, other_put):
    first = info[0] == 0
    early = {}

    def put_early(columns, total):
        early[columns.start] = total

    def put_late(columns, total):
        late = total + added[turn, :, columns]
        own_put(columns, jnp.where(first, early[columns.start], late))
        other_put(columns, jnp.where(first, late, early[columns.start]))

    times(pair, high, low, 0, turn, put_early)
    times(pair, high, low, 1, turn, put_late)


def lead_zero_kernel(lines, info, high, low, added, *refs):
    blocks, (pair, send, cross, chip) = refs[:-4], refs[-4:]
    fill(lines, blocks, pair)
    for turn in range(1, high.shape[1]):

        def own_put(columns, total):
            send[turn - 1, :, columns] = total

        def other_put(columns, total):
            cross[turn - 1, :, columns] = total

        both_times(info, high, low, pair, added, turn, own_put, other_put)
    later = jnp.where(info[0] == 0, 1.0, 0.0)

    def put(columns, total):
        chip[:, columns] = total + later * added[0, :, columns]

    times(pair, high, low, 1 - info[0], 0, put)


def last_kernel(info, high, low, pair, added, keep):
    later = jnp.where(info[0] == 0, 0.0, 1.0)

    def put(columns, total):
        keep[:, columns] = total + later * added[0, :, columns]

    times(pair, high, low, info[0], 0, put)


def total_kernel(info, high, low, pair2, pair1, *refs):
    (*from0, total0) = refs

    def put(columns, total):
        total0[:, columns] = functools.reduce(jnp.add, [total] + [part[:, columns] for part in from0])

    def add(columns, total):
        total0[:, columns] += total

    times(pair2, high, low, 0, 0, put)
    times(pair1, high, low, 1, 0, add)


def pass_kernel(info, *refs):
    count = len(refs) // 2
    for source, target in zip(refs[:count], refs[count:]):
        target[...] = source[...]


def add_kernel(count, info, *refs):
    for terms, out_ref in ((refs[:count], refs[-2]), (refs[count:-2], refs[-1])):
        out_ref[...] = functools.reduce(jnp.add, [term[...] for term in terms])


def finish_kernel(info, own_sum, other_sum, next_own, next_other, *refs):
    (*crossed, out_ref) = refs
    first = info[0] == 0
    sensors, half = out_ref.shape[0], own_sum.shape[0]
    own = own_sum[...] + next_own[...]
    other = functools.reduce(jnp.add, [other_sum[...] + next_other[...]] + [part[...] for part in crossed])
    out_ref[:half, :] = jnp.where(first, own, other)
    out_ref[half:, :] = jnp.where(first, other, own)[2 * half - sensors :, :]


def on_device(model, kernels, lines, rows, spaces):
    core = lax.axis_index("core")
    info = jnp.stack([core, lax.axis_index("space"), lax.axis_index("line"), lax.axis_index("row")]).astype(jnp.int32)
    own_model = model[0]
    depth, columns = own_model.shape
    lags, sensors, width = kernels.shape
    half = -(-sensors // 32) * 16
    block = columns // spaces

    def swap(values):
        return lax.ppermute(values, "core", [(0, 1), (1, 0)])

    def onward(values, target):
        def from_core(source):
            route = [(2 * i + source, 2 * i + 2 + target) for i in range(lines * rows - 1)]
            return lax.ppermute(values, ("line", "row", "core"), route)

        return from_core(target), from_core(1 - target)

    def over_space(sent):
        return [
            lax.ppermute(sent[d - 1], "space", [(i, (i + d) % spaces) for i in range(spaces)])
            for d in range(1, spaces)
        ]

    def over_space_and_core(sent):
        return [
            lax.ppermute(
                sent[d - 1],
                ("core", "space"),
                [(c * spaces + i, (1 - c) * spaces + (i + d) % spaces) for c in range(2) for i in range(spaces)],
            )
            for d in range(1, spaces)
        ]

    kernels_t = jnp.swapaxes(kernels, 1, 2)
    (own_t,) = call(stage_kernel, "stage", [jax.ShapeDtypeStruct(kernels_t.shape, F32)], [info, kernels_t])
    small = jax.ShapeDtypeStruct((half, 2 * width), F32)
    lag_blocks = call(spread_kernel, "spread", [small] * lags, [info, own_t, swap(kernels_t)])

    def shifted(own_block):
        held = {0: own_block, lines: own_block}
        for shift in near_first(lines)[1:]:
            step = 1 if shift <= lines - shift else -1
            held[shift] = lax.ppermute(held[shift - step], "line", [(i, (i + step) % lines) for i in range(lines)])
        moved = [held[shift] for shift in near_first(lines)[1:]]
        return [own_block], moved[:-1], moved[-1:]

    def handed(blocks):
        return [
            lax.ppermute(values, "row", [(i, (i - off) % rows) for i in range(rows)])
            for off in range(1, rows)
            for values in blocks
        ]

    between = max(lines - 2, 0)
    joint = [jax.ShapeDtypeStruct((half * between, 2 * width), F32)] * bool(between)

    pair = jax.ShapeDtypeStruct((2 * half, depth), BF16)
    one = jax.ShapeDtypeStruct((half, block), F32)
    sent = jax.ShapeDtypeStruct((spaces - 1, half, block), F32)
    whole = jax.ShapeDtypeStruct((spaces, half, block), F32)
    flops = 6 * half * depth * block

    own2, near2, far2 = shifted(lag_blocks[2])
    row2 = handed(own2)

    models = [jax.ShapeDtypeStruct((2, spaces, depth, block), BF16)] * 2
    high, low, block1, *staged = call(
        functools.partial(own_halves_kernel, lines, rows),
        "own_halves",
        models + [small] + [jax.ShapeDtypeStruct((depth, block), F32)] * spaces,
        [info, own_model, lag_blocks[1]],
    )
    joint2 = call(join_kernel, "join2", joint, [info, *near2], waits=row2) if joint else []
    high, low = call(
        other_halves_kernel,
        "other_halves",
        models,
        [info, high, low] + [swap(part) for part in staged],
        aliases={1: 0, 2: 1},
    )

    def gathered(own, near, far, row_own, near_joint):
        return own + near + far, ordered(row_own, handed(near_joint), handed(far))

    def ordered(*groups):
        each = [len(group) // (rows - 1) if rows > 1 else 0 for group in groups]
        return [
            group[off * size + at] for off in range(rows - 1) for group, size in zip(groups, each) for at in range(size)
        ]

    line2, row2 = gathered(own2, near2, far2, row2, joint2)
    own1, near1, far1 = shifted(block1)
    row_own1 = handed(own1)
    pair2, send1, *joint1, block0 = call(
        functools.partial(lead_two_kernel, lines, between),
        "lead2",
        [pair, sent] + joint + [small],
        [info, high, low, lag_blocks[0], *line2, *row2, *near1],
        waits=row_own1 + far1,
        flops=flops,
    )
    from1 = over_space(send1)
    line1, row1 = gathered(own1, near1, far1, row_own1, joint1)
    own0, near0, far0 = shifted(block0)
    pair1, send0, *joint0 = call(
        functools.partial(lead_one_kernel, lines, 1 + len(near0)),
        "lead1",
        [pair, sent, jax.ShapeDtypeStruct((half * (1 + len(near0)), 2 * width), F32)],
        [info, high, low, pair2, *line1, *row1, *own0, *near0],
        waits=from1,
        flops=2 * flops,
    )
    from0 = over_space(send0)
    early1, total1 = call(
        rest_one_kernel,
        "rest1",
        [whole, one],
        [info, high, low, pair2, pair1, *from1],
        waits=far0,
        flops=3 * flops,
    )
    line0, row0 = gathered(own0, near0, far0, [], joint0)
    pair0, d_send, d_cross, d_chip = call(
        functools.partial(lead_zero_kernel, lines),
        "lead0",
        [pair, sent, sent, one],
        [info, high, low, early1, *line0, *row0],
        flops=3 * flops,
    )
    d_from, d_from_cross = over_space(d_send), over_space_and_core(d_cross)
    (total0,) = call(total_kernel, "total0", [one], [info, high, low, pair2, pair1, *from0], waits=row0[-1:])
    (passed1,) = call(pass_kernel, "pass1", [one], [info, total1], waits=row0)
    same1, cross1 = onward(passed1, 1)
    same0, cross0 = onward(total0, 0)
    (d_keep,) = call(last_kernel, "last", [one], [info, high, low, pair0, early1], flops=flops)
    owns, others = [d_keep, same1, *d_from], [swap(d_chip), cross1]
    sums = call(functools.partial(add_kernel, len(owns)), "add", [one, one], [info, *owns, *others])
    (result,) = call(
        finish_kernel,
        "finish",
        [jax.ShapeDtypeStruct((sensors, block), F32)],
        [info, *sums, same0, cross0, *d_from_cross],
    )
    return result[None]


def solution(mesh):
    chips, spaces = mesh.shape["tm"] // 2, mesh.shape["space"]
    rows = 1 if chips % 2 else 2
    lines = chips // rows
    grid = Mesh(mesh.devices.reshape(lines, rows, 2, spaces), ("line", "row", "core", "space"))
    return jax.shard_map(
        functools.partial(on_device, lines=lines, rows=rows, spaces=spaces),
        mesh=grid,
        in_specs=(P(("line", "row", "core"), "space", None), P(None, None, ("space", "line", "row", "core"))),
        out_specs=P(("line", "row", "core"), None, "space"),
        check_vma=False,
    )
```

```python
import functools

import jax
import jax.numpy as jnp
from jax import lax
from jax.experimental import pallas as pl
from jax.experimental.pallas import tpu as pltpu
from jax.sharding import Mesh, PartitionSpec as P

F32, BF16 = jnp.float32, jnp.bfloat16
VMEM_LIMIT = 28 * 2**20
SMEM_SPEC = pl.BlockSpec(memory_space=pltpu.SMEM)
VMEM_SPEC = pl.BlockSpec(memory_space=pltpu.VMEM)


def split(values):
    high = values.astype(BF16)
    return high, (values - high.astype(F32)).astype(BF16)


def call(kernel, name, shapes, operands, waits=(), flops=0, aliases=None):
    def body(*refs):
        kernel(*refs[: len(operands)], *refs[len(operands) + len(waits) :])

    return pl.pallas_call(
        body,
        out_shape=shapes,
        in_specs=[SMEM_SPEC] + [VMEM_SPEC] * (len(operands) - 1) + [pl.BlockSpec(memory_space=pl.ANY)] * len(waits),
        out_specs=[VMEM_SPEC] * len(shapes),
        input_output_aliases=aliases or {},
        compiler_params=pltpu.CompilerParams(vmem_limit_bytes=VMEM_LIMIT),
        cost_estimate=pl.CostEstimate(flops=flops, bytes_accessed=1, transcendentals=0),
        name=name,
    )(*operands, *waits)


def stage_kernel(info, source_ref, out_ref):
    out_ref[...] = source_ref[...]


def spread_kernel(info, own_ref, other_ref, *lag_refs):
    first = info[0] == 0
    half = lag_refs[0].shape[0]
    sensors = own_ref.shape[2]
    for lag, out_ref in enumerate(lag_refs):
        own, other = own_ref[lag], other_ref[lag]
        both = jnp.concatenate([jnp.where(first, own, other), jnp.where(first, other, own)], axis=0).T
        out_ref[...] = jnp.where(first, both[:half], both[sensors - half :])


def own_halves_kernel(lines, rows, info, model_ref, next_ref, high_ref, low_ref, next_out, *staged_refs):
    next_out[...] = next_ref[...]
    spaces, depth, block = high_ref.shape[1:]
    width = depth // (lines * rows)
    for turn, staged_ref in enumerate(staged_refs):
        columns = pl.ds(pl.multiple_of(lax.rem(info[1] + turn, spaces) * block, block), block)
        for at in range(lines * rows):
            source = pl.ds(pl.multiple_of(chip_at(at, info, lines, rows) * width, width), width)
            target = slice(at * width, (at + 1) * width)
            values = model_ref[source, columns]
            staged_ref[target, :] = values
            high_ref[info[0], turn, target], low_ref[info[0], turn, target] = split(values)


def other_halves_kernel(info, high_in, low_in, *refs):
    (*staged_refs, high_ref, low_ref) = refs
    for turn, staged_ref in enumerate(staged_refs):
        high_ref[1 - info[0], turn], low_ref[1 - info[0], turn] = split(staged_ref[...])


def near_first(lines):
    return [0] + sorted(range(1, lines), key=lambda shift: (min(shift, lines - shift), shift))


def chip_at(at, info, lines, rows):
    row_off, shift = at // lines, at % lines
    return lax.rem(info[2] - shift + lines, lines) * rows + lax.rem(info[3] + row_off, rows)


def fill(lines, blocks, pair_ref):
    half, width = pair_ref.shape[0] // 2, blocks[0].shape[1]
    count = 0
    for block in blocks:
        for start in range(0, block.shape[0], half):
            at = count // lines * lines + near_first(lines)[count % lines]
            columns = slice(at * width, (at + 1) * width)
            pair_ref[:half, columns], pair_ref[half:, columns] = split(block[start : start + half])
            count += 1


def join_kernel(info, *refs):
    (*parts, out_ref) = refs
    start = 0
    for part in parts:
        out_ref[start : start + part.shape[0]] = part[...]
        start += part.shape[0]


def times(pair_ref, high_ref, low_ref, slot, turn, put):
    half = pair_ref.shape[0] // 2
    width = high_ref.shape[3]
    step = width if width % 256 else 256
    for start in range(0, width, step):
        columns = slice(start, start + step)
        both = jnp.dot(pair_ref[...], high_ref[slot, turn, :, columns], preferred_element_type=F32)
        low = jnp.dot(pair_ref[:half], low_ref[slot, turn, :, columns], preferred_element_type=F32)
        put(columns, both[:half] + (both[half:] + low))


def lead_two_kernel(lines, count, info, high, low, next_block, *refs):
    (*refs, next_out) = refs
    next_out[...] = next_block[...]
    blocks, (pair, send) = lead(lines, count, refs)
    for turn in range(1, high.shape[1]):

        def put(columns, total):
            send[turn - 1, :, columns] = total

        times(pair, high, low, 1, turn, put)


def lead(lines, count, refs):
    if count:
        (*refs, next_out) = refs
    outputs = refs[-2:]
    blocks, between = refs[: len(refs) - count - 2], refs[len(refs) - count - 2 : -2]
    if count:
        join_kernel(None, *between, next_out)
    fill(lines, blocks, outputs[0])
    return blocks, outputs


def lead_one_kernel(lines, count, info, high, low, pair2, *refs):
    blocks, (pair, send) = lead(lines, count, refs)
    for turn in range(1, high.shape[1]):

        def put(columns, total):
            send[turn - 1, :, columns] = total

        def add(columns, total):
            send[turn - 1, :, columns] += total

        times(pair2, high, low, 0, turn, put)
        times(pair, high, low, 1, turn, add)


def rest_one_kernel(info, high, low, pair2, pair1, *refs):
    (*from1, other, total1) = refs

    def put_total(columns, total):
        total1[:, columns] = functools.reduce(jnp.add, [total] + [part[:, columns] for part in from1])

    times(pair2, high, low, 1, 0, put_total)
    for turn in range(high.shape[1]):

        def put(columns, total):
            other[turn, :, columns] = total

        times(pair1, high, low, 0, turn, put)


def both_times(info, high, low, pair, added, turn, own_put, other_put):
    first = info[0] == 0
    early = {}

    def put_early(columns, total):
        early[columns.start] = total

    def put_late(columns, total):
        late = total + added[turn, :, columns]
        own_put(columns, jnp.where(first, early[columns.start], late))
        other_put(columns, jnp.where(first, late, early[columns.start]))

    times(pair, high, low, 0, turn, put_early)
    times(pair, high, low, 1, turn, put_late)


def lead_zero_kernel(lines, info, high, low, added, *refs):
    blocks, (pair, send, cross) = refs[:-3], refs[-3:]
    fill(lines, blocks, pair)
    for turn in range(1, high.shape[1]):

        def own_put(columns, total):
            send[turn - 1, :, columns] = total

        def other_put(columns, total):
            cross[turn - 1, :, columns] = total

        both_times(info, high, low, pair, added, turn, own_put, other_put)


def last_kernel(info, high, low, pair, added, keep):
    later = jnp.where(info[0] == 0, 0.0, 1.0)

    def put(columns, total):
        keep[:, columns] = total + later * added[0, :, columns]

    times(pair, high, low, info[0], 0, put)


def total_kernel(info, high, low, pair2, pair1, pair0, added, *refs):
    (*from0, total0, chip) = refs
    later = jnp.where(info[0] == 0, 1.0, 0.0)

    def put_chip(columns, total):
        chip[:, columns] = total + later * added[0, :, columns]

    times(pair0, high, low, 1 - info[0], 0, put_chip)

    def put(columns, total):
        total0[:, columns] = functools.reduce(jnp.add, [total] + [part[:, columns] for part in from0])

    def add(columns, total):
        total0[:, columns] += total

    times(pair2, high, low, 0, 0, put)
    times(pair1, high, low, 1, 0, add)


def pass_kernel(info, *refs):
    count = len(refs) // 2
    for source, target in zip(refs[:count], refs[count:]):
        target[...] = source[...]


def add_kernel(count, info, *refs):
    for terms, out_ref in ((refs[:count], refs[-2]), (refs[count:-2], refs[-1])):
        out_ref[...] = functools.reduce(jnp.add, [term[...] for term in terms])


def finish_kernel(info, own_sum, other_sum, next_own, next_other, *refs):
    (*crossed, out_ref) = refs
    first = info[0] == 0
    sensors, half = out_ref.shape[0], own_sum.shape[0]
    own = own_sum[...] + next_own[...]
    other = functools.reduce(jnp.add, [other_sum[...] + next_other[...]] + [part[...] for part in crossed])
    out_ref[:half, :] = jnp.where(first, own, other)
    out_ref[half:, :] = jnp.where(first, other, own)[2 * half - sensors :, :]


def on_device(model, kernels, lines, rows, spaces):
    core = lax.axis_index("core")
    info = jnp.stack([core, lax.axis_index("space"), lax.axis_index("line"), lax.axis_index("row")]).astype(jnp.int32)
    own_model = model[0]
    depth, columns = own_model.shape
    lags, sensors, width = kernels.shape
    half = -(-sensors // 32) * 16
    block = columns // spaces

    def swap(values):
        return lax.ppermute(values, "core", [(0, 1), (1, 0)])

    def onward(values, target):
        def from_core(source):
            route = [(2 * i + source, 2 * i + 2 + target) for i in range(lines * rows - 1)]
            return lax.ppermute(values, ("line", "row", "core"), route)

        return from_core(target), from_core(1 - target)

    def over_space(sent):
        return [
            lax.ppermute(sent[d - 1], "space", [(i, (i + d) % spaces) for i in range(spaces)])
            for d in range(1, spaces)
        ]

    def over_space_and_core(sent):
        return [
            lax.ppermute(
                sent[d - 1],
                ("core", "space"),
                [(c * spaces + i, (1 - c) * spaces + (i + d) % spaces) for c in range(2) for i in range(spaces)],
            )
            for d in range(1, spaces)
        ]

    kernels_t = jnp.swapaxes(kernels, 1, 2)
    (own_t,) = call(stage_kernel, "stage", [jax.ShapeDtypeStruct(kernels_t.shape, F32)], [info, kernels_t])
    small = jax.ShapeDtypeStruct((half, 2 * width), F32)
    lag_blocks = call(spread_kernel, "spread", [small] * lags, [info, own_t, swap(kernels_t)])

    def shifted(own_block):
        held = {0: own_block, lines: own_block}
        for shift in near_first(lines)[1:]:
            step = 1 if shift <= lines - shift else -1
            held[shift] = lax.ppermute(held[shift - step], "line", [(i, (i + step) % lines) for i in range(lines)])
        moved = [held[shift] for shift in near_first(lines)[1:]]
        return [own_block], moved[:-1], moved[-1:]

    def handed(blocks):
        return [
            lax.ppermute(values, "row", [(i, (i - off) % rows) for i in range(rows)])
            for off in range(1, rows)
            for values in blocks
        ]

    between = max(lines - 2, 0)
    joint = [jax.ShapeDtypeStruct((half * between, 2 * width), F32)] * bool(between)

    pair = jax.ShapeDtypeStruct((2 * half, depth), BF16)
    one = jax.ShapeDtypeStruct((half, block), F32)
    sent = jax.ShapeDtypeStruct((spaces - 1, half, block), F32)
    whole = jax.ShapeDtypeStruct((spaces, half, block), F32)
    flops = 6 * half * depth * block

    own2, near2, far2 = shifted(lag_blocks[2])
    row2 = handed(own2)

    models = [jax.ShapeDtypeStruct((2, spaces, depth, block), BF16)] * 2
    high, low, block1, *staged = call(
        functools.partial(own_halves_kernel, lines, rows),
        "own_halves",
        models + [small] + [jax.ShapeDtypeStruct((depth, block), F32)] * spaces,
        [info, own_model, lag_blocks[1]],
    )
    joint2 = call(join_kernel, "join2", joint, [info, *near2], waits=row2) if joint else []
    high, low = call(
        other_halves_kernel,
        "other_halves",
        models,
        [info, high, low] + [swap(part) for part in staged],
        aliases={1: 0, 2: 1},
    )

    def gathered(own, near, far, row_own, near_joint):
        return own + near + far, ordered(row_own, handed(near_joint), handed(far))

    def ordered(*groups):
        each = [len(group) // (rows - 1) if rows > 1 else 0 for group in groups]
        return [
            group[off * size + at] for off in range(rows - 1) for group, size in zip(groups, each) for at in range(size)
        ]

    line2, row2 = gathered(own2, near2, far2, row2, joint2)
    own1, near1, far1 = shifted(block1)
    row_own1 = handed(own1)
    pair2, send1, *joint1, block0 = call(
        functools.partial(lead_two_kernel, lines, between),
        "lead2",
        [pair, sent] + joint + [small],
        [info, high, low, lag_blocks[0], *line2, *row2, *near1],
        waits=row_own1 + far1,
        flops=flops,
    )
    from1 = over_space(send1)
    line1, row1 = gathered(own1, near1, far1, row_own1, joint1)
    own0, near0, far0 = shifted(block0)
    pair1, send0, *joint0 = call(
        functools.partial(lead_one_kernel, lines, 1 + len(near0)),
        "lead1",
        [pair, sent, jax.ShapeDtypeStruct((half * (1 + len(near0)), 2 * width), F32)],
        [info, high, low, pair2, *line1, *row1, *own0, *near0],
        waits=from1,
        flops=2 * flops,
    )
    from0 = over_space(send0)
    early1, total1 = call(
        rest_one_kernel,
        "rest1",
        [whole, one],
        [info, high, low, pair2, pair1, *from1],
        waits=far0,
        flops=3 * flops,
    )
    line0, row0 = gathered(own0, near0, far0, [], joint0)
    pair0, d_send, d_cross = call(
        functools.partial(lead_zero_kernel, lines),
        "lead0",
        [pair, sent, sent],
        [info, high, low, early1, *line0, *row0],
        flops=3 * flops,
    )
    d_from, d_from_cross = over_space(d_send), over_space_and_core(d_cross)
    total0, d_chip = call(
        total_kernel, "total0", [one] * 2, [info, high, low, pair2, pair1, pair0, early1, *from0]
    )
    (passed1,) = call(pass_kernel, "pass1", [one], [info, total1], waits=row0)
    same1, cross1 = onward(passed1, 1)
    same0, cross0 = onward(total0, 0)
    (d_keep,) = call(last_kernel, "last", [one], [info, high, low, pair0, early1], flops=flops)
    owns, others = [d_keep, same1, *d_from], [swap(d_chip), cross1]
    sums = call(functools.partial(add_kernel, len(owns)), "add", [one, one], [info, *owns, *others])
    (result,) = call(
        finish_kernel,
        "finish",
        [jax.ShapeDtypeStruct((sensors, block), F32)],
        [info, *sums, same0, cross0, *d_from_cross],
    )
    return result[None]


def solution(mesh):
    chips, spaces = mesh.shape["tm"] // 2, mesh.shape["space"]
    rows = 1 if chips % 2 else 2
    lines = chips // rows
    grid = Mesh(mesh.devices.reshape(lines, rows, 2, spaces), ("line", "row", "core", "space"))
    return jax.shard_map(
        functools.partial(on_device, lines=lines, rows=rows, spaces=spaces),
        mesh=grid,
        in_specs=(P(("line", "row", "core"), "space", None), P(None, None, ("space", "line", "row", "core"))),
        out_specs=P(("line", "row", "core"), None, "space"),
        check_vma=False,
    )
```

```python
import functools

import jax
import jax.numpy as jnp
from jax import lax
from jax.experimental import pallas as pl
from jax.experimental.pallas import tpu as pltpu
from jax.sharding import Mesh, PartitionSpec as P

F32, BF16 = jnp.float32, jnp.bfloat16
VMEM_LIMIT = 28 * 2**20
SMEM_SPEC = pl.BlockSpec(memory_space=pltpu.SMEM)
VMEM_SPEC = pl.BlockSpec(memory_space=pltpu.VMEM)


def split(values):
    high = values.astype(BF16)
    return high, (values - high.astype(F32)).astype(BF16)


def call(kernel, name, shapes, operands, waits=(), flops=0, aliases=None):
    def body(*refs):
        kernel(*refs[: len(operands)], *refs[len(operands) + len(waits) :])

    return pl.pallas_call(
        body,
        out_shape=shapes,
        in_specs=[SMEM_SPEC] + [VMEM_SPEC] * (len(operands) - 1) + [pl.BlockSpec(memory_space=pl.ANY)] * len(waits),
        out_specs=[VMEM_SPEC] * len(shapes),
        input_output_aliases=aliases or {},
        compiler_params=pltpu.CompilerParams(vmem_limit_bytes=VMEM_LIMIT),
        cost_estimate=pl.CostEstimate(flops=flops, bytes_accessed=1, transcendentals=0),
        name=name,
    )(*operands, *waits)


def stage_kernel(info, source_ref, out_ref):
    out_ref[...] = source_ref[...]


def spread_kernel(info, own_ref, other_ref, *lag_refs):
    first = info[0] == 0
    half = lag_refs[0].shape[0]
    sensors = own_ref.shape[2]
    for lag, out_ref in enumerate(lag_refs):
        own, other = own_ref[lag], other_ref[lag]
        both = jnp.concatenate([jnp.where(first, own, other), jnp.where(first, other, own)], axis=0).T
        out_ref[...] = jnp.where(first, both[:half], both[sensors - half :])


def own_halves_kernel(lines, rows, info, model_ref, next_ref, high_ref, low_ref, next_out, *staged_refs):
    next_out[...] = next_ref[...]
    spaces, depth, block = high_ref.shape[1:]
    width = depth // (lines * rows)
    for turn, staged_ref in enumerate(staged_refs):
        columns = pl.ds(pl.multiple_of(lax.rem(info[1] + turn, spaces) * block, block), block)
        for at in range(lines * rows):
            source = pl.ds(pl.multiple_of(chip_at(at, info, lines, rows) * width, width), width)
            target = slice(at * width, (at + 1) * width)
            values = model_ref[source, columns]
            staged_ref[target, :] = values
            high_ref[info[0], turn, target], low_ref[info[0], turn, target] = split(values)


def other_halves_kernel(info, high_in, low_in, *refs):
    (*staged_refs, high_ref, low_ref) = refs
    for turn, staged_ref in enumerate(staged_refs):
        high_ref[1 - info[0], turn], low_ref[1 - info[0], turn] = split(staged_ref[...])


def near_first(lines):
    return [0] + sorted(range(1, lines), key=lambda shift: (min(shift, lines - shift), shift))


def chip_at(at, info, lines, rows):
    row_off, shift = at // lines, at % lines
    return lax.rem(info[2] - shift + lines, lines) * rows + lax.rem(info[3] + row_off, rows)


def fill(lines, blocks, pair_ref):
    half, width = pair_ref.shape[0] // 2, blocks[0].shape[1]
    count = 0
    for block in blocks:
        for start in range(0, block.shape[0], half):
            at = count // lines * lines + near_first(lines)[count % lines]
            columns = slice(at * width, (at + 1) * width)
            pair_ref[:half, columns], pair_ref[half:, columns] = split(block[start : start + half])
            count += 1


def join_kernel(info, *refs):
    (*parts, out_ref) = refs
    start = 0
    for part in parts:
        out_ref[start : start + part.shape[0]] = part[...]
        start += part.shape[0]


def times(pair_ref, high_ref, low_ref, slot, turn, put):
    half = pair_ref.shape[0] // 2
    width = high_ref.shape[3]
    step = width if width % 256 else 256
    for start in range(0, width, step):
        columns = slice(start, start + step)
        both = jnp.dot(pair_ref[...], high_ref[slot, turn, :, columns], preferred_element_type=F32)
        low = jnp.dot(pair_ref[:half], low_ref[slot, turn, :, columns], preferred_element_type=F32)
        put(columns, both[:half] + (both[half:] + low))


def lead_two_kernel(lines, count, info, high, low, next_block, *refs):
    (*refs, next_out) = refs
    next_out[...] = next_block[...]
    blocks, (pair, send) = lead(lines, count, refs)
    for turn in range(1, high.shape[1]):

        def put(columns, total):
            send[turn - 1, :, columns] = total

        times(pair, high, low, 1, turn, put)


def lead(lines, count, refs):
    if count:
        (*refs, next_out) = refs
    outputs = refs[-2:]
    blocks, between = refs[: len(refs) - count - 2], refs[len(refs) - count - 2 : -2]
    if count:
        join_kernel(None, *between, next_out)
    fill(lines, blocks, outputs[0])
    return blocks, outputs


def lead_one_kernel(lines, count, info, high, low, pair2, *refs):
    blocks, (pair, send) = lead(lines, count, refs)
    for turn in range(1, high.shape[1]):

        def put(columns, total):
            send[turn - 1, :, columns] = total

        def add(columns, total):
            send[turn - 1, :, columns] += total

        times(pair2, high, low, 0, turn, put)
        times(pair, high, low, 1, turn, add)


def rest_one_kernel(info, high, low, pair2, pair1, *refs):
    (*from1, other, total1) = refs

    def put_total(columns, total):
        total1[:, columns] = functools.reduce(jnp.add, [total] + [part[:, columns] for part in from1])

    times(pair2, high, low, 1, 0, put_total)
    for turn in range(high.shape[1]):

        def put(columns, total):
            other[turn, :, columns] = total

        times(pair1, high, low, 0, turn, put)


def both_times(info, high, low, pair, added, turn, own_put, other_put):
    first = info[0] == 0
    early = {}

    def put_early(columns, total):
        early[columns.start] = total

    def put_late(columns, total):
        late = total + added[turn, :, columns]
        own_put(columns, jnp.where(first, early[columns.start], late))
        other_put(columns, jnp.where(first, late, early[columns.start]))

    times(pair, high, low, 0, turn, put_early)
    times(pair, high, low, 1, turn, put_late)


def lead_zero_kernel(lines, info, high, low, added, *refs):
    blocks, (pair, send, cross) = refs[:-3], refs[-3:]
    fill(lines, blocks, pair)
    for turn in range(1, high.shape[1]):

        def own_put(columns, total):
            send[turn - 1, :, columns] = total

        def other_put(columns, total):
            cross[turn - 1, :, columns] = total

        both_times(info, high, low, pair, added, turn, own_put, other_put)


def last_kernel(info, high, low, pair, added, keep):
    later = jnp.where(info[0] == 0, 0.0, 1.0)

    def put(columns, total):
        keep[:, columns] = total + later * added[0, :, columns]

    times(pair, high, low, info[0], 0, put)


def total_kernel(info, high, low, pair2, pair1, pair0, added, *refs):
    (*from0, total0, chip) = refs
    later = jnp.where(info[0] == 0, 1.0, 0.0)

    def put_chip(columns, total):
        chip[:, columns] = total + later * added[0, :, columns]

    times(pair0, high, low, 1 - info[0], 0, put_chip)

    def put(columns, total):
        total0[:, columns] = functools.reduce(jnp.add, [total] + [part[:, columns] for part in from0])

    def add(columns, total):
        total0[:, columns] += total

    times(pair2, high, low, 0, 0, put)
    times(pair1, high, low, 1, 0, add)


def pass_kernel(info, *refs):
    count = len(refs) // 2
    for source, target in zip(refs[:count], refs[count:]):
        target[...] = source[...]


def add_kernel(count, info, *refs):
    for terms, out_ref in ((refs[:count], refs[-2]), (refs[count:-2], refs[-1])):
        out_ref[...] = functools.reduce(jnp.add, [term[...] for term in terms])


def finish_kernel(info, own_sum, other_sum, next_own, next_other, *refs):
    (*crossed, out_ref) = refs
    first = info[0] == 0
    sensors, half = out_ref.shape[0], own_sum.shape[0]
    own = own_sum[...] + next_own[...]
    other = functools.reduce(jnp.add, [other_sum[...] + next_other[...]] + [part[...] for part in crossed])
    out_ref[:half, :] = jnp.where(first, own, other)
    out_ref[half:, :] = jnp.where(first, other, own)[2 * half - sensors :, :]


def on_device(model, kernels, lines, rows, spaces):
    core = lax.axis_index("core")
    info = jnp.stack([core, lax.axis_index("space"), lax.axis_index("line"), lax.axis_index("row")]).astype(jnp.int32)
    own_model = model[0]
    depth, columns = own_model.shape
    lags, sensors, width = kernels.shape
    half = -(-sensors // 32) * 16
    block = columns // spaces

    def swap(values):
        return lax.ppermute(values, "core", [(0, 1), (1, 0)])

    def onward(values, target):
        def from_core(source):
            route = [(2 * i + source, 2 * i + 2 + target) for i in range(lines * rows - 1)]
            return lax.ppermute(values, ("line", "row", "core"), route)

        return from_core(target), from_core(1 - target)

    def over_space(sent):
        return [
            lax.ppermute(sent[d - 1], "space", [(i, (i + d) % spaces) for i in range(spaces)])
            for d in range(1, spaces)
        ]

    def over_space_and_core(sent):
        return [
            lax.ppermute(
                sent[d - 1],
                ("core", "space"),
                [(c * spaces + i, (1 - c) * spaces + (i + d) % spaces) for c in range(2) for i in range(spaces)],
            )
            for d in range(1, spaces)
        ]

    kernels_t = jnp.swapaxes(kernels, 1, 2)
    (own_t,) = call(stage_kernel, "stage", [jax.ShapeDtypeStruct(kernels_t.shape, F32)], [info, kernels_t])
    small = jax.ShapeDtypeStruct((half, 2 * width), F32)
    lag_blocks = call(spread_kernel, "spread", [small] * lags, [info, own_t, swap(kernels_t)])

    def shifted(own_block):
        held = {0: own_block, lines: own_block}
        for shift in near_first(lines)[1:]:
            step = 1 if shift <= lines - shift else -1
            held[shift] = lax.ppermute(held[shift - step], "line", [(i, (i + step) % lines) for i in range(lines)])
        moved = [held[shift] for shift in near_first(lines)[1:]]
        return [own_block], moved[:-1], moved[-1:]

    def handed(blocks):
        return [
            lax.ppermute(values, "row", [(i, (i - off) % rows) for i in range(rows)])
            for off in range(1, rows)
            for values in blocks
        ]

    between = max(lines - 2, 0)
    joint = [jax.ShapeDtypeStruct((half * between, 2 * width), F32)] * bool(between)

    pair = jax.ShapeDtypeStruct((2 * half, depth), BF16)
    one = jax.ShapeDtypeStruct((half, block), F32)
    sent = jax.ShapeDtypeStruct((spaces - 1, half, block), F32)
    whole = jax.ShapeDtypeStruct((spaces, half, block), F32)
    flops = 6 * half * depth * block

    own2, near2, far2 = shifted(lag_blocks[2])
    row2 = handed(own2)

    models = [jax.ShapeDtypeStruct((2, spaces, depth, block), BF16)] * 2
    high, low, block1, *staged = call(
        functools.partial(own_halves_kernel, lines, rows),
        "own_halves",
        models + [small] + [jax.ShapeDtypeStruct((depth, block), F32)] * spaces,
        [info, own_model, lag_blocks[1]],
    )
    joint2 = call(join_kernel, "join2", joint, [info, *near2], waits=row2) if joint else []
    high, low = call(
        other_halves_kernel,
        "other_halves",
        models,
        [info, high, low] + [swap(part) for part in staged],
        aliases={1: 0, 2: 1},
    )

    def gathered(own, near, far, row_own, near_joint):
        return own + near + far, ordered(row_own, handed(near_joint), handed(far))

    def ordered(*groups):
        each = [len(group) // (rows - 1) if rows > 1 else 0 for group in groups]
        return [
            group[off * size + at] for off in range(rows - 1) for group, size in zip(groups, each) for at in range(size)
        ]

    line2, row2 = gathered(own2, near2, far2, row2, joint2)
    own1, near1, far1 = shifted(block1)
    row_own1 = handed(own1)
    pair2, send1, *joint1, block0 = call(
        functools.partial(lead_two_kernel, lines, between),
        "lead2",
        [pair, sent] + joint + [small],
        [info, high, low, lag_blocks[0], *line2, *row2, *near1],
        waits=row_own1 + far1,
        flops=flops,
    )
    from1 = over_space(send1)
    line1, row1 = gathered(own1, near1, far1, row_own1, joint1)
    own0, near0, far0 = shifted(block0)
    pair1, send0, *joint0 = call(
        functools.partial(lead_one_kernel, lines, 1 + len(near0)),
        "lead1",
        [pair, sent, jax.ShapeDtypeStruct((half * (1 + len(near0)), 2 * width), F32)],
        [info, high, low, pair2, *line1, *row1, *own0, *near0],
        waits=from1,
        flops=2 * flops,
    )
    from0 = over_space(send0)
    early1, total1 = call(
        rest_one_kernel,
        "rest1",
        [whole, one],
        [info, high, low, pair2, pair1, *from1],
        waits=far0,
        flops=3 * flops,
    )
    line0, row0 = gathered(own0, near0, far0, [], joint0)
    pair0, d_send, d_cross = call(
        functools.partial(lead_zero_kernel, lines),
        "lead0",
        [pair, sent, sent],
        [info, high, low, early1, *line0, *row0],
        flops=3 * flops,
    )
    d_from, d_from_cross = over_space(d_send), over_space_and_core(d_cross)
    total0, d_chip = call(
        total_kernel, "total0", [one] * 2, [info, high, low, pair2, pair1, pair0, early1, *from0]
    )
    same1, cross1 = onward(total1, 1)
    same0, cross0 = onward(total0, 0)
    (d_keep,) = call(last_kernel, "last", [one], [info, high, low, pair0, early1], flops=flops)
    owns, others = [d_keep, same1, *d_from], [swap(d_chip), cross1]
    sums = call(functools.partial(add_kernel, len(owns)), "add", [one, one], [info, *owns, *others])
    (result,) = call(
        finish_kernel,
        "finish",
        [jax.ShapeDtypeStruct((sensors, block), F32)],
        [info, *sums, same0, cross0, *d_from_cross],
    )
    return result[None]


def solution(mesh):
    chips, spaces = mesh.shape["tm"] // 2, mesh.shape["space"]
    rows = 1 if chips % 2 else 2
    lines = chips // rows
    grid = Mesh(mesh.devices.reshape(lines, rows, 2, spaces), ("line", "row", "core", "space"))
    return jax.shard_map(
        functools.partial(on_device, lines=lines, rows=rows, spaces=spaces),
        mesh=grid,
        in_specs=(P(("line", "row", "core"), "space", None), P(None, None, ("space", "line", "row", "core"))),
        out_specs=P(("line", "row", "core"), None, "space"),
        check_vma=False,
    )
```
